512 devices in a mesh: tile: 32 (over y, x), plane: 16 (over z, core).
Axes of the slice: x: 4, y: 8, z: 8, core: 2. Of those that a mesh axis runs over, the one named last changes fastest.
Arguments:
- slab_data: bfloat16 [512, 128, 2048], P('tile', 'plane'), may hold values from -24 to 24
- footprints: float32 [32768, 256], P(('tile', 'plane')), may hold values from 0 to 4
- traces: float32 [32768, 128], P(('tile', 'plane')), may hold values from -6 to 6
- corners: int32 [32768, 2], P(('tile', 'plane')), may hold values from 0 to 112, as said below
- counts: int32 [512], P(('tile', 'plane')), may hold values from 32 to 64, as said below
Outputs:
- updated_footprints: float32 [32768, 256], P(('tile', 'plane'))
The draws below stay inside these ranges and needn't reach their ends.
Inputs may be any that keep to these rules, and one draw needn't show every extreme that they name: corners[n, 0] lies in 0 to 112 and corners[n, 1] in 0 to 15, so a box may run into the next tile; both ends are taken in every draw. `counts`: some owner has 64 live neurons and some has 32 in every draw.
All inputs are finite; a program needn't handle non-finite values.
Results may differ from the reference program's by a relative error of at most 0.0028.
Values may be sent and summed in bfloat16 or wider, within the bound.
A program may use at most 192 MiB of HBM per device.

```python
import jax
import jax.numpy as jnp
from jax import lax

ROWS = 128
COLS = 16
F = 128
K_DEV = 64
PR = 16
PC = 16
SWEEPS = 2
GROUPS = 2
NROW = 2048
NCOL = 512
OWNERS = 512
NEURONS = 32768
N_TILE = 32
N_PLANE = 16


def draw_corners(key, part):
    key = jax.random.fold_in(key, 11)
    first, second, third, fourth = jax.random.split(key, 4)
    top_rows = jax.random.randint(first, (NEURONS,), 0, ROWS - PR + 1)
    left_columns = jax.random.randint(second, (NEURONS,), 0, COLS)
    top_rows = top_rows.at[jax.random.randint(third, (), 0, NEURONS)].set(ROWS - PR)
    left_columns = left_columns.at[jax.random.randint(fourth, (), 0, NEURONS)].set(COLS - 1)
    return jnp.stack([top_rows, left_columns], axis=1).astype(jnp.int32)


def draw_counts(key, part):
    key = jax.random.fold_in(key, 23)
    first, second, third = jax.random.split(key, 3)
    values = jax.random.randint(first, (OWNERS,), K_DEV // 2, K_DEV + 1)
    fullest = jax.random.randint(second, (), 0, OWNERS)
    emptiest = (fullest + 1 + jax.random.randint(third, (), 0, OWNERS - 1)) % OWNERS
    values = values.at[fullest].set(K_DEV)
    values = values.at[emptiest].set(K_DEV // 2)
    return values.astype(jnp.int32)


def level_of(rng, shape, shards, least, top_value):
    loudness = 1.0
    for axis_at, blocks in shards:
        steps = jax.random.uniform(jax.random.fold_in(jax.random.fold_in(rng, 6), axis_at), (blocks,), jnp.float32, least / len(shards), top_value / len(shards))
        loudness = loudness * jnp.repeat(jnp.exp(steps), shape[axis_at] // blocks).reshape((-1,) + (1,) * (len(shape) - 1 - axis_at))
    return loudness


def normal_values(key, shape, scale, bound, cuts=(), held_as=jnp.bfloat16):
    drawn = jax.random.normal(key, shape, jnp.float32) * scale
    if len(cuts) > 0:
        drawn = level_of(key, shape, cuts, -0.22, 0.18) * drawn
    return jnp.clip(drawn, min=-bound, max=bound).astype(held_as)


def setup_inputs(seed: int = 0) -> dict:
    seeds = jax.random.split(jax.random.key(seed), 6)
    slab_data = normal_values(seeds[0], (NCOL, F, NROW), 4.0, 24.0, ((0, 32), (1, 16)))
    footprints = jnp.clip(4.0 * jax.random.uniform(seeds[1], (NEURONS, PR * PC), jnp.float32) ** level_of(seeds[1], (NEURONS, PR * PC), ((0, 512),), -0.2, 0.2), 0.0, 4.0)
    traces = normal_values(seeds[2], (NEURONS, F), 1.0, 6.0, ((0, 512),), jnp.float32)
    corners = draw_corners(jax.random.fold_in(seeds[5], 71), 0)
    counts = draw_counts(jax.random.fold_in(seeds[5], 71), 0)
    return dict(slab_data=slab_data, footprints=footprints, traces=traces, corners=corners, counts=counts)


def update_region(data_block, patches, trace_rows, top_rows, left_columns, alive_flags):
    column_count, row_count = data_block.shape[0], data_block.shape[2]
    slot_count, patch_rows, patch_columns = patches.shape
    row_hit = (jnp.arange(row_count)[None, :, None] == top_rows[:, None, None] + jnp.arange(patch_rows)[None, None, :]).astype(jnp.float32) * alive_flags[:, None, None]
    column_hit = (jnp.arange(column_count)[None, :, None] == left_columns[:, None, None] + jnp.arange(patch_columns)[None, None, :]).astype(jnp.float32)
    spread = jnp.einsum('sij,scj->sic', patches, column_hit, precision=lax.Precision.HIGHEST)
    current = jnp.einsum('sri,sic->rcs', row_hit, spread, precision=lax.Precision.HIGHEST).reshape(row_count * column_count, slot_count)
    support = (jnp.sum(row_hit, axis=2).T[:, None, :] * jnp.sum(column_hit, axis=2).T[None, :, :]).reshape(row_count * column_count, slot_count)
    signal = jnp.einsum('cfr,sf->rcs', data_block, trace_rows.astype(jnp.bfloat16), preferred_element_type=jnp.float32).reshape(row_count * column_count, slot_count)
    gram = jnp.dot(trace_rows, trace_rows.T, precision=lax.Precision.HIGHEST)
    scaling = jnp.where(alive_flags > 0.5, jnp.diagonal(gram), jnp.ones_like(alive_flags))
    group_width = slot_count // (2 * GROUPS)
    split_shape = (row_count * column_count, 2, GROUPS, group_width)
    signal_blocks = signal.reshape(split_shape)
    support_blocks = support.reshape(split_shape)
    scale_blocks = scaling.reshape(2, GROUPS, group_width)
    gram_blocks = gram.reshape(slot_count, 2, GROUPS, group_width)
    for repeat_index in range(SWEEPS):
        for group_index in range(GROUPS):
            columns_used = gram_blocks[:, :, group_index, :].reshape(slot_count, 2 * group_width)
            mixed = jnp.dot(current, columns_used, precision=lax.Precision.HIGHEST).reshape(row_count * column_count, 2, group_width)
            blocked = current.reshape(split_shape)
            fresh = support_blocks[:, :, group_index, :] * jnp.maximum(blocked[:, :, group_index, :] + (signal_blocks[:, :, group_index, :] - mixed) / scale_blocks[:, group_index, :], 0.0)
            current = blocked.at[:, :, group_index, :].set(fresh).reshape(row_count * column_count, slot_count)
    current = current.reshape(row_count, column_count, slot_count)
    picked = jnp.einsum('sri,rcs->sic', row_hit, current, precision=lax.Precision.HIGHEST)
    return jnp.einsum('sic,scj->sij', picked, column_hit, precision=lax.Precision.HIGHEST)


def reference(slab_data, footprints, traces, corners, counts):
    owner_count = N_TILE * N_PLANE
    local_index = jnp.arange(K_DEV, dtype=jnp.int32)
    patch_all = footprints.reshape(owner_count, K_DEV, PR, PC)
    trace_all = traces.reshape(owner_count, K_DEV, F)
    corner_all = corners.reshape(owner_count, K_DEV, 2)
    alive_all = (local_index[None, :] < counts[:, None]).astype(jnp.float32)
    zero_index = jnp.zeros((), jnp.int32)

    def one_owner(owner):
        tile_index = (owner // N_PLANE).astype(jnp.int32)
        band_index = (owner % N_PLANE).astype(jnp.int32)
        data_block = lax.dynamic_slice(slab_data, (tile_index * COLS, zero_index, band_index * ROWS), (COLS, F, ROWS))
        left_owner = jnp.maximum(owner - N_PLANE, 0).astype(jnp.int32)
        has_left = (tile_index > 0).astype(jnp.float32)
        slot_patch = jnp.concatenate([patch_all[left_owner], patch_all[owner]], axis=0)
        slot_trace = jnp.concatenate([trace_all[left_owner], trace_all[owner]], axis=0)
        top_rows = jnp.concatenate([corner_all[left_owner, :, 0], corner_all[owner, :, 0]], axis=0).astype(jnp.int32)
        left_columns = jnp.concatenate([corner_all[left_owner, :, 1] - COLS, corner_all[owner, :, 1]], axis=0).astype(jnp.int32)
        alive_flags = jnp.concatenate([alive_all[left_owner] * has_left, alive_all[owner]], axis=0)
        pieces = update_region(data_block, slot_patch, slot_trace, top_rows, left_columns, alive_flags)
        return pieces[:K_DEV], pieces[K_DEV:]

    left_parts, own_parts = lax.map(one_owner, jnp.arange(owner_count, dtype=jnp.int32))
    following = jnp.concatenate([left_parts[N_PLANE:], jnp.zeros((N_PLANE, K_DEV, PR, PC), jnp.float32)], axis=0)
    return (own_parts + following).reshape(owner_count * K_DEV, PR * PC)
```

```python
import functools

import jax
import jax.numpy as jnp
from jax import lax
from jax.experimental import pallas as pl
from jax.experimental.pallas import tpu as pltpu
from jax.sharding import PartitionSpec as P

PR = 16
PC = 16
SWEEPS = 2
GROUPS = 2
CHUNK = 4
MESH = pl.DeviceIdType.MESH
GONE = 1 << 14


def mixed_order(left, own):
    half = own.shape[0] // GROUPS
    parts = []
    for g in range(GROUPS):
        parts += [left[g * half : (g + 1) * half], own[g * half : (g + 1) * half]]
    return jnp.concatenate(parts, axis=0)


def unmixed(x):
    quarter = x.shape[0] // (2 * GROUPS)
    blocks = [x[i * quarter : (i + 1) * quarter] for i in range(2 * GROUPS)]
    return jnp.concatenate(blocks[0::2], axis=0), jnp.concatenate(blocks[1::2], axis=0)


def column_of(row):
    n = row.shape[1]
    eye = lax.broadcasted_iota(jnp.int32, (n, n), 0) == lax.broadcasted_iota(jnp.int32, (n, n), 1)
    spread = jnp.where(eye, jnp.broadcast_to(row.astype(jnp.float32), (n, n)), 0.0)
    return jnp.sum(spread, axis=1, keepdims=True).astype(jnp.int32)


def split(x):
    high = x.astype(jnp.bfloat16)
    return high, (x - high.astype(jnp.float32)).astype(jnp.bfloat16)


def kernel(
    n_tile, n_plane, slab, fp, tr, corners, counts, own_out, ret_out,
    buf, own_fp, nb_fp, own_tr, nb_tr, own_corner, own_meta, nb_meta, own_count,
    patch, dense, base_s, step_s, weights, pieces, left_piece,
    load_sem, send_sem, recv_sem, side_send, side_recv, ret_send, ret_recv,
):
    cols, rows = buf.shape[1], buf.shape[3]
    slots = own_fp.shape[0]
    n_chunk = cols // CHUNK
    tile, me = lax.axis_index("tile"), lax.axis_index("plane")
    right = lax.rem(tile + 1, n_tile)
    left = lax.rem(tile + n_tile - 1, n_tile)

    barrier = pltpu.get_barrier_semaphore()

    @pl.loop(1, n_plane)
    def _(k):
        pl.semaphore_signal(
            barrier, inc=1, device_id={"plane": lax.rem(me + k, n_plane)}, device_id_type=MESH
        )

    for other in (left, right):
        pl.semaphore_signal(barrier, inc=1, device_id={"tile": other}, device_id_type=MESH)
    pl.semaphore_wait(barrier, n_plane + 1)

    def side(i, src, dst):
        return pltpu.make_async_remote_copy(
            src, dst, side_send.at[i], side_recv.at[i], device_id={"tile": right}, device_id_type=MESH
        )

    side_fp, side_tr = side(0, fp, nb_fp), side(1, tr, nb_tr)
    side_meta = side(2, own_meta, nb_meta)
    side_fp.start()
    side_tr.start()
    loads = [
        pltpu.make_async_copy(src, dst, load_sem.at[i])
        for i, (src, dst) in enumerate(
            ((corners, own_corner), (counts, own_count), (tr, own_tr), (fp, own_fp))
        )
    ]
    for load in loads:
        load.start()

    @pl.loop(0, n_chunk)
    def _(q):
        columns = pl.ds(q * CHUNK, CHUNK)

        @pl.loop(1, n_plane)
        def _(k):
            peer = lax.rem(me + k, n_plane)
            pltpu.make_async_remote_copy(
                slab.at[columns, :, pl.ds(pl.multiple_of(peer * rows, rows), rows)],
                buf.at[me, columns],
                send_sem.at[q],
                recv_sem.at[q],
                device_id={"plane": peer},
                device_id_type=MESH,
            ).start()

        pltpu.make_async_copy(
            slab.at[columns, :, pl.ds(pl.multiple_of(me * rows, rows), rows)],
            buf.at[me, columns],
            recv_sem.at[q],
        ).start()

    loads[0].wait()
    loads[1].wait()
    lane = lax.broadcasted_iota(jnp.int32, (1, slots), 1)
    own_meta[...] = jnp.zeros_like(own_meta)
    own_meta[0:1, 0:slots] = own_corner[0:1, :]
    own_meta[1:2, 0:slots] = jnp.where(lane < own_count[0, 0], own_corner[1:2, :], GONE)
    side_meta.start()
    loads[2].wait()
    loads[3].wait()
    side_meta.wait_recv()
    side_tr.wait_recv()
    side_fp.wait_recv()

    gone = jnp.where(tile > 0, -cols, GONE)
    top = mixed_order(column_of(nb_meta[0:1, 0:slots]), column_of(own_meta[0:1, 0:slots]))
    first = mixed_order(
        column_of(nb_meta[1:2, 0:slots]) + gone, column_of(own_meta[1:2, 0:slots])
    )
    alive = first < cols
    patch[...] = mixed_order(nb_fp[...], own_fp[...])
    trace = mixed_order(nb_tr[...], own_tr[...])
    both = 2 * slots
    gram = lax.dot_general(
        trace, trace, (((1,), (1,)), ((), ())),
        precision=lax.Precision.HIGHEST, preferred_element_type=jnp.float32,
    )
    eye = lax.broadcasted_iota(jnp.int32, (both, both), 0) == lax.broadcasted_iota(
        jnp.int32, (both, both), 1
    )
    diagonal = jnp.sum(jnp.where(eye, gram, 0.0), axis=1, keepdims=True)
    scale = jnp.where(alive, diagonal, 1.0)
    high, low = split(jnp.where(eye, 0.0, gram) / scale)
    for g in range(GROUPS):
        at = slice(g * slots, (g + 1) * slots)
        weights[g, 0:slots, 0:both] = high[at]
        weights[g, 0:slots, both : 2 * both] = high[at]
        weights[g, slots:both, 0:both] = low[at]
        weights[g, slots:both, both : 2 * both] = jnp.zeros((slots, both), jnp.bfloat16)
    trace_bf = trace.astype(jnp.bfloat16)
    inverse = jnp.broadcast_to(1.0 / scale, (both, rows))

    row = lax.broadcasted_iota(jnp.int32, (both, rows), 1)
    i_at = row - top
    in_rows = (i_at >= 0) & (i_at < PR)
    base_s[...] = jnp.where(in_rows, i_at, -1)
    step_s[...] = jnp.broadcast_to(first, (both, rows))

    def box_of(c):
        i_of = base_s[...]
        j_of = c - step_s[...]
        inside = (i_of >= 0) & (j_of >= 0) & (j_of < PC)
        return i_of, j_of, inside

    @pl.loop(0, cols)
    def _(c):
        i_of, j_of, inside = box_of(c)
        at = (i_of & 7) * PC + (j_of & (PC - 1))
        lower = jnp.take_along_axis(patch[:, 0:128], at, axis=1)
        upper = jnp.take_along_axis(patch[:, 128:256], at, axis=1)
        dense[c] = jnp.where(inside, jnp.where(i_of >= 8, upper, lower), 0.0)

    pieces[...] = jnp.zeros_like(pieces)
    lane_row = lax.broadcasted_iota(jnp.int32, (both, 128), 1)
    j_lane = lane_row & (PC - 1)
    pick_low = jnp.broadcast_to(top, (both, 128)) + (lane_row >> 4)

    @pl.loop(0, n_chunk)
    def _(q):
        c0 = q * CHUNK
        landed = buf.at[:, pl.ds(c0, CHUNK)]
        pltpu.make_async_copy(landed, landed, recv_sem.at[q]).wait()
        data, signal, now = [], [], []
        for c in range(CHUNK):
            block = buf[:, c0 + c].astype(jnp.float32)
            data.append(block.reshape(-1, rows).astype(jnp.bfloat16))
        summed = jnp.dot(
            trace_bf, jnp.concatenate(data, axis=1), preferred_element_type=jnp.float32
        )
        for c in range(CHUNK):
            _, _, inside = box_of(c0 + c)
            signal.append(
                jnp.where(inside, summed[:, c * rows : (c + 1) * rows] * inverse, -jnp.inf)
            )
            now.append(dense[c0 + c])
        signal = jnp.concatenate(signal, axis=1)
        now = jnp.concatenate(now, axis=1)
        now = [now[g * slots : (g + 1) * slots] for g in range(GROUPS)]
        parts = [split(x) for x in now]
        for _ in range(SWEEPS):
            for g in range(GROUPS):
                stacked = jnp.concatenate([p[0] for p in parts] + [p[1] for p in parts], axis=0)
                product = jnp.dot(weights[g], stacked, preferred_element_type=jnp.float32)
                mixed = product[0:slots] + product[slots:both]
                now[g] = jnp.maximum(signal[g * slots : (g + 1) * slots] - mixed, 0.0)
                parts[g] = split(now[g])
        done = jnp.concatenate(now, axis=0)
        for c in range(CHUNK):
            at = done[:, c * rows : (c + 1) * rows]
            hit = (c0 + c) - step_s[...] == j_lane
            for h in range(2):
                got = jnp.take_along_axis(at, pick_low + 8 * h, axis=1)
                where = slice(h * 128, (h + 1) * 128)
                pieces[:, where] = jnp.where(hit, got, pieces[:, where])

    for_left, own = unmixed(pieces[...])
    left_piece[...] = for_left
    back = pltpu.make_async_remote_copy(
        left_piece, ret_out, ret_send, ret_recv, device_id={"tile": left}, device_id_type=MESH
    )
    back.start()
    own_out[...] = own
    for copy in (side_fp, side_tr, side_meta):
        copy.wait_send()

    @pl.loop(0, n_chunk)
    def _(q):
        gone_out = buf.at[pl.ds(0, n_plane - 1), pl.ds(q * CHUNK, CHUNK)]
        pltpu.make_async_copy(gone_out, gone_out, send_sem.at[q]).wait()

    back.wait()


def body(slab_data, footprints, traces, corners, counts):
    n_tile, n_plane = lax.axis_size("tile"), lax.axis_size("plane")
    cols, frames, rows = slab_data.shape
    rows = rows // n_plane
    slots, box = footprints.shape
    span = traces.shape[1]
    both = 2 * slots
    any_space = pl.BlockSpec(memory_space=pltpu.HBM)
    vmem = pl.BlockSpec(memory_space=pltpu.VMEM)
    f32, bf16, i32 = jnp.float32, jnp.bfloat16, jnp.int32
    own, returned = pl.pallas_call(
        functools.partial(kernel, n_tile, n_plane),
        out_shape=(
            jax.ShapeDtypeStruct((slots, box), f32),
            jax.ShapeDtypeStruct((slots, box), f32),
        ),
        in_specs=[any_space] * 5,
        out_specs=(vmem, vmem),
        scratch_shapes=[
            pltpu.VMEM((n_plane, cols, frames, rows), bf16),
            pltpu.VMEM((slots, box), f32),
            pltpu.VMEM((slots, box), f32),
            pltpu.VMEM((slots, span), f32),
            pltpu.VMEM((slots, span), f32),
            pltpu.VMEM((2, slots), i32),
            pltpu.VMEM((8, 128), i32),
            pltpu.VMEM((8, 128), i32),
            pltpu.SMEM((1, 1), i32),
            pltpu.VMEM((both, box), f32),
            pltpu.VMEM((cols, both, rows), f32),
            pltpu.VMEM((both, rows), i32),
            pltpu.VMEM((both, rows), i32),
            pltpu.VMEM((GROUPS, both, 2 * both), bf16),
            pltpu.VMEM((both, box), f32),
            pltpu.VMEM((slots, box), f32),
            pltpu.SemaphoreType.DMA((4,)),
            pltpu.SemaphoreType.DMA((cols // CHUNK,)),
            pltpu.SemaphoreType.DMA((cols // CHUNK,)),
            pltpu.SemaphoreType.DMA((3,)),
            pltpu.SemaphoreType.DMA((3,)),
            pltpu.SemaphoreType.DMA,
            pltpu.SemaphoreType.DMA,
        ],
        compiler_params=pltpu.CompilerParams(
            collective_id=0, has_side_effects=True, vmem_limit_bytes=32 << 20
        ),
    )(slab_data, footprints, traces, corners.T, counts.reshape(1, 1))
    return own + returned


def solution(mesh):
    in_specs = (
        P("tile", "plane", None),
        P(("tile", "plane"), None),
        P(("tile", "plane"), None),
        P(("tile", "plane"), None),
        P(("tile", "plane")),
    )
    out_specs = P(("tile", "plane"), None)
    return jax.shard_map(body, mesh=mesh, in_specs=in_specs, out_specs=out_specs, check_vma=False)
```

```python
import functools

import jax
import jax.numpy as jnp
from jax import lax
from jax.experimental import pallas as pl
from jax.experimental.pallas import tpu as pltpu
from jax.sharding import PartitionSpec as P

PR = 16
PC = 16
SWEEPS = 2
GROUPS = 2
CHUNKS = ((0, 4), (4, 4), (8, 4), (12, 3), (15, 1))
LAST_LEFT = 3
X_SIZE = 4
LANES = 128
MESH = pl.DeviceIdType.MESH
GONE = 1 << 14


def mixed_order(left, own):
    half = own.shape[0] // GROUPS
    parts = []
    for g in range(GROUPS):
        parts += [left[g * half : (g + 1) * half], own[g * half : (g + 1) * half]]
    return jnp.concatenate(parts, axis=0)


def column_of(row):
    n = row.shape[1]
    eye = lax.broadcasted_iota(jnp.int32, (n, n), 0) == lax.broadcasted_iota(jnp.int32, (n, n), 1)
    spread = jnp.where(eye, jnp.broadcast_to(row.astype(jnp.float32), (n, n)), 0.0)
    return jnp.sum(spread, axis=1, keepdims=True).astype(jnp.int32)


def split(x):
    high = x.astype(jnp.bfloat16)
    return high, (x - high.astype(jnp.float32)).astype(jnp.bfloat16)


def kernel(
    n_tile, n_plane, slab, fp, tr, corners, counts, own_out, ret_out,
    buf, own_fp, nb_fp, own_tr, nb_tr, own_corner, own_meta, nb_meta, own_count,
    patch, first_mixed, later_high, later_low, row_at, first_at, pick_at, inverse_at,
    weights, trace_bf, left_piece,
    load_sem, send_sem, recv_sem, side_send, side_recv, ret_send, ret_recv, plane_in, side_in,
):
    cols, rows = buf.shape[1], buf.shape[3]
    slots = own_fp.shape[0]
    both = 2 * slots
    quarter = slots // GROUPS
    tile, me = lax.axis_index("tile"), lax.axis_index("plane")
    has_left, has_right = tile > 0, tile < n_tile - 1
    half = n_plane // 2
    place = jnp.where(me == 0, half - 1, jnp.where(me < half, me - 1, me))

    def plane_at(k):
        return jnp.where(k < half - 1, k + 1, jnp.where(k == half - 1, 0, k))

    left_first = has_left & (lax.rem(tile, X_SIZE) != 0)
    left_second = has_left & (lax.rem(tile, X_SIZE) == 0)
    right_second = has_right & (lax.rem(tile + 1, X_SIZE) != 0)
    right_first = has_right & (lax.rem(tile + 1, X_SIZE) == 0)

    barrier = pltpu.get_barrier_semaphore()

    @pl.loop(place + 1, n_plane)
    def _(k):
        pl.semaphore_signal(
            barrier, inc=1, device_id={"plane": plane_at(k)}, device_id_type=MESH
        )

    @pl.when(right_second)
    def _():
        pl.semaphore_signal(barrier, inc=1, device_id={"tile": tile + 1}, device_id_type=MESH)

    @pl.when(left_second)
    def _():
        pl.semaphore_signal(barrier, inc=1, device_id={"tile": tile - 1}, device_id_type=MESH)

    loads = [
        pltpu.make_async_copy(src, dst, load_sem.at[i])
        for i, (src, dst) in enumerate(
            ((corners, own_corner), (counts, own_count), (tr, own_tr), (fp, own_fp))
        )
    ]
    for load in loads:
        load.start()
    for q, (c0, n) in enumerate(CHUNKS):
        pltpu.make_async_copy(
            slab.at[pl.ds(c0, n), :, pl.ds(pl.multiple_of(me * rows, rows), rows)],
            buf.at[me, pl.ds(c0, n)],
            recv_sem.at[q],
        ).start()

    before = place + left_first.astype(jnp.int32) + right_first.astype(jnp.int32)

    @pl.when(before > 0)
    def _():
        pl.semaphore_wait(barrier, before)

    @pl.loop(0, place)
    def _(k):
        pl.semaphore_signal(
            plane_in.at[me], inc=1, device_id={"plane": plane_at(k)}, device_id_type=MESH
        )

    @pl.when(left_first)
    def _():
        pl.semaphore_signal(side_in.at[1], inc=1, device_id={"tile": tile - 1}, device_id_type=MESH)

    @pl.when(right_first)
    def _():
        pl.semaphore_signal(side_in.at[0], inc=1, device_id={"tile": tile + 1}, device_id_type=MESH)

    def send(q, peer):
        c0, n = CHUNKS[q]
        pltpu.make_async_remote_copy(
            slab.at[pl.ds(c0, n), :, pl.ds(pl.multiple_of(peer * rows, rows), rows)],
            buf.at[me, pl.ds(c0, n)],
            send_sem.at[q],
            recv_sem.at[q],
            device_id={"plane": peer},
            device_id_type=MESH,
        ).start()

    early = jnp.minimum(place, half)
    for a, b in ((0, early), (early, place)):
        for q in range(len(CHUNKS)):

            @pl.loop(a, b)
            def _(k, q=q):
                send(q, plane_at(k))

    def side(i, src, dst):
        return pltpu.make_async_remote_copy(
            src, dst, side_send.at[i], side_recv.at[i],
            device_id={"tile": tile + 1}, device_id_type=MESH,
        )

    side_fp, side_tr = side(0, fp, nb_fp), side(1, tr, nb_tr)
    side_meta = side(2, own_meta, nb_meta)
    loads[0].wait()
    loads[1].wait()
    lane = lax.broadcasted_iota(jnp.int32, (1, slots), 1)
    own_meta[...] = jnp.zeros_like(own_meta)
    own_meta[0:1, 0:slots] = own_corner[0:1, :]
    own_meta[1:2, 0:slots] = jnp.where(lane < own_count[0, 0], own_corner[1:2, :], GONE)

    @pl.when(right_second)
    def _():
        pl.semaphore_wait(side_in.at[1], 1)

    @pl.when(has_right)
    def _():
        side_meta.start()
        side_tr.start()
        side_fp.start()

    @pl.loop(place + 1, n_plane)
    def _(k):
        peer = plane_at(k)
        pl.semaphore_wait(plane_in.at[peer], 1)
        for q in range(len(CHUNKS)):
            send(q, peer)

    loads[2].wait()
    loads[3].wait()

    @pl.when(has_left)
    def _():
        side_meta.wait_recv()
        side_tr.wait_recv()
        side_fp.wait_recv()

    @pl.when(jnp.logical_not(has_left))
    def _():
        nb_meta[...] = jnp.full(nb_meta.shape, GONE, jnp.int32)
        nb_tr[...] = jnp.zeros_like(nb_tr)
        nb_fp[...] = jnp.zeros_like(nb_fp)

    top = mixed_order(column_of(nb_meta[0:1, 0:slots]), column_of(own_meta[0:1, 0:slots]))
    first = mixed_order(
        column_of(nb_meta[1:2, 0:slots]) - cols, column_of(own_meta[1:2, 0:slots])
    )
    alive = first < cols
    patch[...] = mixed_order(nb_fp[...], own_fp[...])
    trace = mixed_order(nb_tr[...], own_tr[...])
    gram = lax.dot_general(
        trace, trace, (((1,), (1,)), ((), ())),
        precision=lax.Precision.HIGHEST, preferred_element_type=jnp.float32,
    )
    eye = lax.broadcasted_iota(jnp.int32, (both, both), 0) == lax.broadcasted_iota(
        jnp.int32, (both, both), 1
    )
    diagonal = jnp.sum(jnp.where(eye, gram, 0.0), axis=1, keepdims=True)
    scale = jnp.where(alive, diagonal, 1.0)
    high, low = split(jnp.where(eye, 0.0, gram) / scale)
    for g in range(GROUPS):
        at = slice(g * slots, (g + 1) * slots)
        weights[g, 0:slots, 0:both] = high[at]
        weights[g, 0:slots, both : 2 * both] = high[at]
        weights[g, slots:both, 0:both] = low[at]
        weights[g, slots:both, both : 2 * both] = jnp.zeros((slots, both), jnp.bfloat16)
    trace_bf[...] = trace.astype(jnp.bfloat16)
    inverse_at[...] = jnp.broadcast_to(1.0 / scale, (both, rows))

    i_at = lax.broadcasted_iota(jnp.int32, (both, rows), 1) - top
    row_at[...] = jnp.where((i_at >= 0) & (i_at < PR), i_at, -1)
    first_at[...] = jnp.broadcast_to(first, (both, rows))
    lane_row = lax.broadcasted_iota(jnp.int32, (both, LANES), 1)
    pick_at[...] = jnp.broadcast_to(top, (both, LANES)) + (lane_row >> 4)

    def box_of(c):
        i_of = row_at[...]
        j_of = c - first_at[...]
        return i_of, j_of, (i_of >= 0) & (j_of >= 0) & (j_of < PC)

    def multiply(g, parts):
        stacked = jnp.concatenate([p[0] for p in parts] + [p[1] for p in parts], axis=0)
        product = jnp.dot(weights[g], stacked, preferred_element_type=jnp.float32)
        return product[0:slots] + product[slots:both]

    @pl.loop(0, cols // 2)
    def _(pair):
        highs, lows = [], []
        for c in (2 * pair, 2 * pair + 1):
            i_of, j_of, inside = box_of(c)
            at = (i_of & 7) * PC + (j_of & (PC - 1))
            lower = jnp.take_along_axis(patch[:, 0:LANES], at, axis=1)
            upper = jnp.take_along_axis(patch[:, LANES : 2 * LANES], at, axis=1)
            high, low = split(jnp.where(inside, jnp.where(i_of >= 8, upper, lower), 0.0))
            later_high[c] = high[slots:both]
            later_low[c] = low[slots:both]
            highs.append(high)
            lows.append(low)
        mixed = multiply(0, [(jnp.concatenate(highs, axis=1), jnp.concatenate(lows, axis=1))])
        first_mixed[2 * pair] = mixed[:, 0:rows]
        first_mixed[2 * pair + 1] = mixed[:, rows : 2 * rows]

    left_piece[...] = jnp.zeros_like(left_piece)
    own_out[...] = jnp.zeros_like(own_out)

    def take_back(c0, n, done, side_index, target):
        for g in range(GROUPS):
            a = g * slots + side_index * quarter
            j_lane = lax.broadcasted_iota(jnp.int32, (quarter, LANES), 1) & (PC - 1)
            for h in range(2):
                where = (slice(g * quarter, (g + 1) * quarter), slice(h * LANES, (h + 1) * LANES))
                sofar = target[where]
                for c in range(n):
                    got = jnp.take_along_axis(
                        done[a : a + quarter, c * rows : (c + 1) * rows],
                        pick_at[a : a + quarter, :] + 8 * h,
                        axis=1,
                    )
                    sofar = jnp.where(c0 + c - first_at[a : a + quarter, :] == j_lane, got, sofar)
                target[where] = sofar

    back = pltpu.make_async_remote_copy(
        left_piece, ret_out, ret_send, ret_recv, device_id={"tile": tile - 1}, device_id_type=MESH
    )
    for q, (c0, n) in enumerate(CHUNKS):
        landed = buf.at[:, pl.ds(c0, n)]
        pltpu.make_async_copy(landed, landed, recv_sem.at[q]).wait()
        data, signal = [], []
        for c in range(c0, c0 + n):
            block = buf[:, c].astype(jnp.float32)
            data.append(block.reshape(-1, rows).astype(jnp.bfloat16))
        summed = jnp.dot(
            trace_bf[...], jnp.concatenate(data, axis=1), preferred_element_type=jnp.float32
        )
        for c in range(n):
            _, _, inside = box_of(c0 + c)
            signal.append(
                jnp.where(inside, summed[:, c * rows : (c + 1) * rows] * inverse_at[...], -jnp.inf)
            )
        signal = jnp.concatenate(signal, axis=1)
        signal = [signal[g * slots : (g + 1) * slots] for g in range(GROUPS)]
        wide = lambda ref: jnp.concatenate([ref[c] for c in range(c0, c0 + n)], axis=1)
        now = [None] * GROUPS
        parts = [None] + [(wide(later_high), wide(later_low))]
        mixed = wide(first_mixed)
        for step in range(SWEEPS * GROUPS):
            g = step % GROUPS
            if step > 0:
                mixed = multiply(g, parts)
            now[g] = jnp.maximum(signal[g] - mixed, 0.0)
            parts[g] = split(now[g])
        done = jnp.concatenate(now, axis=0)
        if q <= LAST_LEFT:
            take_back(c0, n, done, 0, left_piece)
        if q == LAST_LEFT:

            @pl.when(left_second)
            def _():
                pl.semaphore_wait(side_in.at[0], 1)

            @pl.when(has_left)
            def _():
                back.start()

        take_back(c0, n, done, 1, own_out)

    @pl.when(has_right)
    def _():
        for copy in (side_fp, side_tr, side_meta):
            copy.wait_send()

    @pl.when(jnp.logical_not(has_right))
    def _():
        ret_out[...] = jnp.zeros_like(ret_out)

    for q, (c0, n) in enumerate(CHUNKS):
        gone_out = buf.at[pl.ds(0, n_plane - 1), pl.ds(c0, n)]
        pltpu.make_async_copy(gone_out, gone_out, send_sem.at[q]).wait()

    @pl.when(has_left)
    def _():
        back.wait_send()

    @pl.when(has_right)
    def _():
        back.wait_recv()


def body(slab_data, footprints, traces, corners, counts):
    n_tile, n_plane = lax.axis_size("tile"), lax.axis_size("plane")
    cols, frames, rows = slab_data.shape
    rows = rows // n_plane
    slots, box = footprints.shape
    span = traces.shape[1]
    both = 2 * slots
    hbm = pl.BlockSpec(memory_space=pltpu.HBM)
    vmem = pl.BlockSpec(memory_space=pltpu.VMEM)
    f32, bf16, i32 = jnp.float32, jnp.bfloat16, jnp.int32
    dma = pltpu.SemaphoreType.DMA
    regular = pltpu.SemaphoreType.REGULAR
    own, returned = pl.pallas_call(
        functools.partial(kernel, n_tile, n_plane),
        out_shape=(
            pltpu.VMEM((slots, box), f32),
            pltpu.VMEM((slots, box), f32),
        ),
        in_specs=[hbm] * 5,
        out_specs=(vmem, vmem),
        scratch_shapes=[
            pltpu.VMEM((n_plane, cols, frames, rows), bf16),
            pltpu.VMEM((slots, box), f32),
            pltpu.VMEM((slots, box), f32),
            pltpu.VMEM((slots, span), f32),
            pltpu.VMEM((slots, span), f32),
            pltpu.VMEM((2, slots), i32),
            pltpu.VMEM((8, 128), i32),
            pltpu.VMEM((8, 128), i32),
            pltpu.SMEM((1, 1), i32),
            pltpu.VMEM((both, box), f32),
            pltpu.VMEM((cols, slots, rows), f32),
            pltpu.VMEM((cols, slots, rows), bf16),
            pltpu.VMEM((cols, slots, rows), bf16),
            pltpu.VMEM((both, rows), i32),
            pltpu.VMEM((both, rows), i32),
            pltpu.VMEM((both, LANES), i32),
            pltpu.VMEM((both, rows), f32),
            pltpu.VMEM((GROUPS, both, 2 * both), bf16),
            pltpu.VMEM((both, span), bf16),
            pltpu.VMEM((slots, box), f32),
            dma((4,)),
            dma((len(CHUNKS),)),
            dma((len(CHUNKS),)),
            dma((3,)),
            dma((3,)),
            dma,
            dma,
            regular((n_plane,)),
            regular((2,)),
        ],
        compiler_params=pltpu.CompilerParams(
            collective_id=0, has_side_effects=True, vmem_limit_bytes=60 << 20
        ),
    )(slab_data, footprints, traces, corners.T, counts.reshape(1, 1))
    return own + returned


def solution(mesh):
    in_specs = (
        P("tile", "plane", None),
        P(("tile", "plane"), None),
        P(("tile", "plane"), None),
        P(("tile", "plane"), None),
        P(("tile", "plane")),
    )
    out_specs = P(("tile", "plane"), None)
    return jax.shard_map(body, mesh=mesh, in_specs=in_specs, out_specs=out_specs, check_vma=False)
```

```python
import functools

import jax
import jax.numpy as jnp
from jax import lax
from jax.experimental import pallas as pl
from jax.experimental.pallas import tpu as pltpu
from jax.sharding import PartitionSpec as P

PR = 16
PC = 16
SWEEPS = 2
GROUPS = 2
CHUNKS = ((0, 8), (8, 4), (12, 4))
BLOCK = 4
X_SIZE = 4
LANES = 128
MESH = pl.DeviceIdType.MESH
GONE = 1 << 14


def mixed_order(left, own):
    half = own.shape[0] // GROUPS
    parts = []
    for g in range(GROUPS):
        parts += [left[g * half : (g + 1) * half], own[g * half : (g + 1) * half]]
    return jnp.concatenate(parts, axis=0)


def column_of(row):
    n = row.shape[1]
    eye = lax.broadcasted_iota(jnp.int32, (n, n), 0) == lax.broadcasted_iota(jnp.int32, (n, n), 1)
    spread = jnp.where(eye, jnp.broadcast_to(row.astype(jnp.float32), (n, n)), 0.0)
    return jnp.sum(spread, axis=1, keepdims=True).astype(jnp.int32)


def split(x):
    high = x.astype(jnp.bfloat16)
    return high, (x - high.astype(jnp.float32)).astype(jnp.bfloat16)


def kernel(
    n_tile, n_plane, slab, fp, tr, corners, counts, out,
    buf, own_fp, nb_fp, own_tr, nb_tr, own_corner, own_meta, nb_meta, own_count,
    patch, first_mixed, later_high, later_low, row_at, first_at, pick_at, inverse_at,
    weights, trace_bf, own_piece, left_piece, ret_piece,
    load_sem, send_sem, recv_sem, side_send, side_recv, ret_send, ret_recv, plane_in, side_in,
):
    cols, rows = buf.shape[1], buf.shape[3]
    slots = own_fp.shape[0]
    both = 2 * slots
    quarter = slots // GROUPS
    tile, me = lax.axis_index("tile"), lax.axis_index("plane")
    has_left, has_right = tile > 0, tile < n_tile - 1
    half = n_plane // 2
    place = jnp.where(me == 0, half - 1, jnp.where(me < half, me - 1, me))

    def plane_at(k):
        return jnp.where(k < half - 1, k + 1, jnp.where(k == half - 1, 0, k))

    left_first = has_left & (lax.rem(tile, X_SIZE) != 0)
    left_second = has_left & (lax.rem(tile, X_SIZE) == 0)
    right_second = has_right & (lax.rem(tile + 1, X_SIZE) != 0)
    right_first = has_right & (lax.rem(tile + 1, X_SIZE) == 0)

    barrier = pltpu.get_barrier_semaphore()

    @pl.loop(place + 1, n_plane)
    def _(k):
        pl.semaphore_signal(
            barrier, inc=1, device_id={"plane": plane_at(k)}, device_id_type=MESH
        )

    @pl.when(right_second)
    def _():
        pl.semaphore_signal(barrier, inc=1, device_id={"tile": tile + 1}, device_id_type=MESH)

    @pl.when(left_second)
    def _():
        pl.semaphore_signal(barrier, inc=1, device_id={"tile": tile - 1}, device_id_type=MESH)

    loads = [
        pltpu.make_async_copy(src, dst, load_sem.at[i])
        for i, (src, dst) in enumerate(
            ((corners, own_corner), (counts, own_count), (tr, own_tr), (fp, own_fp))
        )
    ]
    for load in loads:
        load.start()
    before = place + left_first.astype(jnp.int32) + right_first.astype(jnp.int32)

    @pl.when(before > 0)
    def _():
        pl.semaphore_wait(barrier, before)

    @pl.loop(0, place)
    def _(k):
        pl.semaphore_signal(
            plane_in.at[me], inc=1, device_id={"plane": plane_at(k)}, device_id_type=MESH
        )

    @pl.when(left_first)
    def _():
        pl.semaphore_signal(side_in.at[1], inc=1, device_id={"tile": tile - 1}, device_id_type=MESH)

    @pl.when(right_first)
    def _():
        pl.semaphore_signal(side_in.at[0], inc=1, device_id={"tile": tile + 1}, device_id_type=MESH)

    def send(q, peer):
        c0, n = CHUNKS[q]
        pltpu.make_async_remote_copy(
            slab.at[pl.ds(c0, n), :, pl.ds(pl.multiple_of(peer * rows, rows), rows)],
            buf.at[me, pl.ds(c0, n)],
            send_sem.at[q],
            recv_sem.at[q],
            device_id={"plane": peer},
            device_id_type=MESH,
        ).start()

    late = place >= half
    early = jnp.minimum(place, half)
    for a, b in ((0, 2), (2, half), (half, n_plane)):
        for q in range(len(CHUNKS)):

            @pl.loop(jnp.minimum(a, place), jnp.minimum(b, place))
            def _(k, q=q):
                send(q, jnp.where(late, k, plane_at(k)))

    for q, (c0, n) in enumerate(CHUNKS):
        pltpu.make_async_copy(
            slab.at[pl.ds(c0, n), :, pl.ds(pl.multiple_of(me * rows, rows), rows)],
            buf.at[me, pl.ds(c0, n)],
            recv_sem.at[q],
        ).start()

    def side(i, src, dst):
        return pltpu.make_async_remote_copy(
            src, dst, side_send.at[i], side_recv.at[i],
            device_id={"tile": tile + 1}, device_id_type=MESH,
        )

    side_fp, side_tr = side(0, fp, nb_fp), side(1, tr, nb_tr)
    side_meta = side(2, own_meta, nb_meta)
    loads[0].wait()
    loads[1].wait()
    lane = lax.broadcasted_iota(jnp.int32, (1, slots), 1)
    own_meta[...] = jnp.zeros_like(own_meta)
    own_meta[0:1, 0:slots] = own_corner[0:1, :]
    own_meta[1:2, 0:slots] = jnp.where(lane < own_count[0, 0], own_corner[1:2, :], GONE)

    @pl.when(right_second)
    def _():
        pl.semaphore_wait(side_in.at[1], 1)

    @pl.when(has_right)
    def _():
        side_meta.start()
        side_tr.start()
        side_fp.start()

    @pl.loop(place + 1, n_plane)
    def _(k):
        peer = plane_at(k)
        pl.semaphore_wait(plane_in.at[peer], 1)
        for q in range(len(CHUNKS)):
            send(q, peer)

    loads[2].wait()
    loads[3].wait()

    @pl.when(has_left)
    def _():
        side_meta.wait_recv()
        side_tr.wait_recv()
        side_fp.wait_recv()

    @pl.when(jnp.logical_not(has_left))
    def _():
        nb_meta[...] = jnp.full(nb_meta.shape, GONE, jnp.int32)
        nb_tr[...] = jnp.zeros_like(nb_tr)
        nb_fp[...] = jnp.zeros_like(nb_fp)

    top = mixed_order(column_of(nb_meta[0:1, 0:slots]), column_of(own_meta[0:1, 0:slots]))
    first = mixed_order(
        column_of(nb_meta[1:2, 0:slots]) - cols, column_of(own_meta[1:2, 0:slots])
    )
    alive = first < cols
    patch[...] = mixed_order(nb_fp[...], own_fp[...])
    trace = mixed_order(nb_tr[...], own_tr[...])
    gram = lax.dot_general(
        trace, trace, (((1,), (1,)), ((), ())),
        precision=lax.Precision.HIGHEST, preferred_element_type=jnp.float32,
    )
    eye = lax.broadcasted_iota(jnp.int32, (both, both), 0) == lax.broadcasted_iota(
        jnp.int32, (both, both), 1
    )
    diagonal = jnp.sum(jnp.where(eye, gram, 0.0), axis=1, keepdims=True)
    scale = jnp.where(alive, diagonal, 1.0)
    high, low = split(jnp.where(eye, 0.0, gram) / scale)
    for g in range(GROUPS):
        at = slice(g * slots, (g + 1) * slots)
        weights[g, 0:slots, 0:both] = high[at]
        weights[g, 0:slots, both : 2 * both] = high[at]
        weights[g, slots:both, 0:both] = low[at]
        weights[g, slots:both, both : 2 * both] = jnp.zeros((slots, both), jnp.bfloat16)
    trace_bf[...] = trace.astype(jnp.bfloat16)
    inverse_at[...] = jnp.broadcast_to(1.0 / scale, (both, rows))

    i_at = lax.broadcasted_iota(jnp.int32, (both, rows), 1) - top
    row_at[...] = jnp.where((i_at >= 0) & (i_at < PR), i_at, -1)
    first_at[...] = jnp.broadcast_to(first, (both, rows))
    lane_row = lax.broadcasted_iota(jnp.int32, (both, LANES), 1)
    pick_at[...] = jnp.broadcast_to(top, (both, LANES)) + (lane_row & (PR - 1))

    def box_of(c):
        i_of = row_at[...]
        j_of = c - first_at[...]
        return i_of, j_of, (i_of >= 0) & (j_of >= 0) & (j_of < PC)

    def multiply(g, parts):
        stacked = jnp.concatenate([p[0] for p in parts] + [p[1] for p in parts], axis=0)
        product = jnp.dot(weights[g], stacked, preferred_element_type=jnp.float32)
        return product[0:slots] + product[slots:both]

    @pl.loop(0, cols // 2)
    def _(pair):
        highs, lows = [], []
        for c in (2 * pair, 2 * pair + 1):
            i_of, j_of, inside = box_of(c)
            at = (i_of & 7) * PC + (j_of & (PC - 1))
            lower = jnp.take_along_axis(patch[:, 0:LANES], at, axis=1)
            upper = jnp.take_along_axis(patch[:, LANES : 2 * LANES], at, axis=1)
            high, low = split(jnp.where(inside, jnp.where(i_of >= 8, upper, lower), 0.0))
            later_high[c] = high[slots:both]
            later_low[c] = low[slots:both]
            highs.append(high)
            lows.append(low)
        mixed = multiply(0, [(jnp.concatenate(highs, axis=1), jnp.concatenate(lows, axis=1))])
        first_mixed[2 * pair] = mixed[:, 0:rows]
        first_mixed[2 * pair + 1] = mixed[:, rows : 2 * rows]

    lane = lax.broadcasted_iota(jnp.int32, (quarter, LANES), 1)
    lane_spot = lane >> 4

    def take_back(c0, n, done, which, target):
        kept = target[c0 // BLOCK] if c0 % BLOCK else jnp.zeros((quarter, LANES), jnp.float32)
        for g in range(GROUPS):
            a = g * slots + which * quarter
            for c in range(n):
                got = jnp.take_along_axis(
                    done[a : a + quarter, c * rows : (c + 1) * rows],
                    pick_at[a : a + quarter, :],
                    axis=1,
                )
                kept = jnp.where(lane_spot == g * BLOCK + (c0 + c) % BLOCK, got, kept)
        target[c0 // BLOCK] = kept

    def back(b):
        return pltpu.make_async_remote_copy(
            left_piece.at[b], ret_piece.at[b], ret_send.at[b], ret_recv.at[b],
            device_id={"tile": tile - 1}, device_id_type=MESH,
        )

    def place_back(b, pieces, sofar):
        new = []
        for g in range(GROUPS):
            a = g * slots + quarter
            for h in range(2):
                column = first_at[a : a + quarter, :] + (lane & (PC - 1))
                at = g * (BLOCK * PR) + (column & (BLOCK - 1)) * PR + (lane >> 4) + 8 * h
                got = jnp.take_along_axis(pieces, at, axis=1)
                new.append(jnp.where((column >> 2) == b, got, sofar[g * 2 + h]))
        return new

    n_block = cols // BLOCK
    boxes = [jnp.zeros((quarter, LANES), jnp.float32)] * (2 * GROUPS)
    for c0 in range(0, cols, BLOCK):
        n = BLOCK
        for q, (start, width) in enumerate(CHUNKS):
            if start == c0:
                landed = buf.at[:, pl.ds(start, width)]
                pltpu.make_async_copy(landed, landed, recv_sem.at[q]).wait()
        data, signal = [], []
        for c in range(c0, c0 + n):
            block = buf[:, c].astype(jnp.float32)
            data.append(block.reshape(-1, rows).astype(jnp.bfloat16))
        summed = jnp.dot(
            trace_bf[...], jnp.concatenate(data, axis=1), preferred_element_type=jnp.float32
        )
        for c in range(n):
            _, _, inside = box_of(c0 + c)
            signal.append(
                jnp.where(inside, summed[:, c * rows : (c + 1) * rows] * inverse_at[...], -jnp.inf)
            )
        signal = jnp.concatenate(signal, axis=1)
        signal = [signal[g * slots : (g + 1) * slots] for g in range(GROUPS)]
        wide = lambda ref: jnp.concatenate([ref[c] for c in range(c0, c0 + n)], axis=1)
        now = [None] * GROUPS
        parts = [None] + [(wide(later_high), wide(later_low))]
        mixed = wide(first_mixed)
        for step in range(SWEEPS * GROUPS):
            g = step % GROUPS
            if step > 0:
                mixed = multiply(g, parts)
            now[g] = jnp.maximum(signal[g] - mixed, 0.0)
            parts[g] = split(now[g])
        done = jnp.concatenate(now, axis=0)
        if True:
            take_back(c0, n, done, 0, left_piece)
        if c0 == 0:

            @pl.when(left_second)
            def _():
                pl.semaphore_wait(side_in.at[0], 1)

        if (c0 + n) % BLOCK == 0:

            @pl.when(has_left)
            def _(b=c0 // BLOCK):
                back(b).start()

        take_back(c0, n, done, 1, own_piece)
        if (c0 + n) % BLOCK == 0:
            boxes = place_back(c0 // BLOCK, own_piece[c0 // BLOCK], boxes)

    @pl.when(has_right)
    def _():
        for copy in (side_fp, side_tr, side_meta):
            copy.wait_send()

    @pl.when(jnp.logical_not(has_right))
    def _():
        ret_piece[...] = jnp.zeros_like(ret_piece)

    for b in range(n_block):

        @pl.when(has_right)
        def _(b=b):
            back(b).wait_recv()

        boxes = place_back(n_block + b, ret_piece[b], boxes)
    for g in range(GROUPS):
        for h in range(2):
            out[g * quarter : (g + 1) * quarter, h * LANES : (h + 1) * LANES] = boxes[g * 2 + h]

    for q, (c0, n) in enumerate(CHUNKS):
        gone_out = buf.at[pl.ds(0, n_plane - 1), pl.ds(c0, n)]
        pltpu.make_async_copy(gone_out, gone_out, send_sem.at[q]).wait()

    @pl.when(has_left)
    def _():
        for b in range(n_block):
            back(b).wait_send()


def body(slab_data, footprints, traces, corners, counts):
    n_tile, n_plane = lax.axis_size("tile"), lax.axis_size("plane")
    cols, frames, rows = slab_data.shape
    rows = rows // n_plane
    slots, box = footprints.shape
    span = traces.shape[1]
    both = 2 * slots
    hbm = pl.BlockSpec(memory_space=pltpu.HBM)
    vmem = pl.BlockSpec(memory_space=pltpu.VMEM)
    f32, bf16, i32 = jnp.float32, jnp.bfloat16, jnp.int32
    dma = pltpu.SemaphoreType.DMA
    regular = pltpu.SemaphoreType.REGULAR
    return pl.pallas_call(
        functools.partial(kernel, n_tile, n_plane),
        out_shape=pltpu.VMEM((slots, box), f32),
        in_specs=[hbm] * 5,
        out_specs=vmem,
        scratch_shapes=[
            pltpu.VMEM((n_plane, cols, frames, rows), bf16),
            pltpu.VMEM((slots, box), f32),
            pltpu.VMEM((slots, box), f32),
            pltpu.VMEM((slots, span), f32),
            pltpu.VMEM((slots, span), f32),
            pltpu.VMEM((2, slots), i32),
            pltpu.VMEM((8, 128), i32),
            pltpu.VMEM((8, 128), i32),
            pltpu.SMEM((1, 1), i32),
            pltpu.VMEM((both, box), f32),
            pltpu.VMEM((cols, slots, rows), f32),
            pltpu.VMEM((cols, slots, rows), bf16),
            pltpu.VMEM((cols, slots, rows), bf16),
            pltpu.VMEM((both, rows), i32),
            pltpu.VMEM((both, rows), i32),
            pltpu.VMEM((both, LANES), i32),
            pltpu.VMEM((both, rows), f32),
            pltpu.VMEM((GROUPS, both, 2 * both), bf16),
            pltpu.VMEM((both, span), bf16),
            pltpu.VMEM((cols // BLOCK, slots // GROUPS, LANES), f32),
            pltpu.VMEM((cols // BLOCK, slots // GROUPS, LANES), f32),
            pltpu.VMEM((cols // BLOCK, slots // GROUPS, LANES), f32),
            dma((4,)),
            dma((len(CHUNKS),)),
            dma((len(CHUNKS),)),
            dma((3,)),
            dma((3,)),
            dma((cols // BLOCK,)),
            dma((cols // BLOCK,)),
            regular((n_plane,)),
            regular((2,)),
        ],
        compiler_params=pltpu.CompilerParams(
            collective_id=0, has_side_effects=True, vmem_limit_bytes=60 << 20
        ),
    )(slab_data, footprints, traces, corners.T, counts.reshape(1, 1))


def solution(mesh):
    in_specs = (
        P("tile", "plane", None),
        P(("tile", "plane"), None),
        P(("tile", "plane"), None),
        P(("tile", "plane"), None),
        P(("tile", "plane")),
    )
    out_specs = P(("tile", "plane"), None)
    return jax.shard_map(body, mesh=mesh, in_specs=in_specs, out_specs=out_specs, check_vma=False)
```

```python
import functools

import jax
import jax.numpy as jnp
from jax import lax
from jax.experimental import pallas as pl
from jax.experimental.pallas import tpu as pltpu
from jax.sharding import PartitionSpec as P

PR = 16
PC = 16
SWEEPS = 2
GROUPS = 2
CHUNKS = ((0, 8), (8, 4), (12, 4))
BLOCK = 4
X_SIZE = 4
LANES = 128
MESH = pl.DeviceIdType.MESH
GONE = 1 << 14


def mixed_order(left, own):
    half = own.shape[0] // GROUPS
    parts = []
    for g in range(GROUPS):
        parts += [left[g * half : (g + 1) * half], own[g * half : (g + 1) * half]]
    return jnp.concatenate(parts, axis=0)


def column_of(row):
    n = row.shape[1]
    eye = lax.broadcasted_iota(jnp.int32, (n, n), 0) == lax.broadcasted_iota(jnp.int32, (n, n), 1)
    spread = jnp.where(eye, jnp.broadcast_to(row.astype(jnp.float32), (n, n)), 0.0)
    return jnp.sum(spread, axis=1, keepdims=True).astype(jnp.int32)


def split(x):
    high = x.astype(jnp.bfloat16)
    return high, (x - high.astype(jnp.float32)).astype(jnp.bfloat16)


def kernel(
    n_tile, n_plane, slab, fp, tr, corners, counts, out,
    buf, own_fp, nb_fp, own_tr, nb_tr, own_corner, own_meta, nb_meta, own_count,
    patch, first_mixed, later_high, later_low, row_at, first_at, pick_at, inverse_at,
    weights, trace_bf, own_piece, left_piece, ret_piece,
    load_sem, send_sem, recv_sem, side_send, side_recv, ret_send, ret_recv, plane_in, side_in, relay,
):
    cols, rows = buf.shape[1], buf.shape[3]
    slots = own_fp.shape[0]
    both = 2 * slots
    quarter = slots // GROUPS
    tile, me = lax.axis_index("tile"), lax.axis_index("plane")
    has_left, has_right = tile > 0, tile < n_tile - 1
    half = n_plane // 2
    place = jnp.where(me == 0, half - 1, jnp.where(me < half, me - 1, me))

    late = place >= half

    def plane_at(k):
        return jnp.where(k < half - 1, k + 1, jnp.where(k == half - 1, 0, k))

    left_first = has_left & (lax.rem(tile, X_SIZE) != 0)
    left_second = has_left & (lax.rem(tile, X_SIZE) == 0)
    right_second = has_right & (lax.rem(tile + 1, X_SIZE) != 0)
    right_first = has_right & (lax.rem(tile + 1, X_SIZE) == 0)

    barrier = pltpu.get_barrier_semaphore()

    @pl.loop(place + 1, n_plane)
    def _(k):
        pl.semaphore_signal(
            barrier, inc=1, device_id={"plane": plane_at(k)}, device_id_type=MESH
        )

    @pl.when(right_second)
    def _():
        pl.semaphore_signal(barrier, inc=1, device_id={"tile": tile + 1}, device_id_type=MESH)

    @pl.when(left_second & jnp.logical_not(late))
    def _():
        pl.semaphore_signal(barrier, inc=1, device_id={"tile": tile - 1}, device_id_type=MESH)

    loads = [
        pltpu.make_async_copy(src, dst, load_sem.at[i])
        for i, (src, dst) in enumerate(
            ((corners, own_corner), (counts, own_count), (tr, own_tr), (fp, own_fp))
        )
    ]
    for load in loads:
        load.start()
    right_told = right_first & jnp.logical_not(late)
    before = place + left_first.astype(jnp.int32) + right_told.astype(jnp.int32)

    @pl.when(before > 0)
    def _():
        pl.semaphore_wait(barrier, before)

    @pl.loop(0, place)
    def _(k):
        pl.semaphore_signal(
            plane_in.at[me], inc=1, device_id={"plane": plane_at(k)}, device_id_type=MESH
        )

    @pl.when(left_first)
    def _():
        pl.semaphore_signal(side_in.at[1], inc=1, device_id={"tile": tile - 1}, device_id_type=MESH)

    @pl.when(right_told)
    def _():
        pl.semaphore_signal(side_in.at[0], inc=1, device_id={"tile": tile + 1}, device_id_type=MESH)

    def send(q, peer):
        c0, n = CHUNKS[q]
        pltpu.make_async_remote_copy(
            slab.at[pl.ds(c0, n), :, pl.ds(pl.multiple_of(peer * rows, rows), rows)],
            buf.at[me, pl.ds(c0, n)],
            send_sem.at[q],
            recv_sem.at[q],
            device_id={"plane": peer},
            device_id_type=MESH,
        ).start()

    early = jnp.minimum(place, half)
    for a, b in ((0, 2), (2, half), (half, n_plane)):
        for q in range(len(CHUNKS)):

            @pl.loop(jnp.minimum(a, place), jnp.minimum(b, place))
            def _(k, q=q):
                send(q, jnp.where(late, k, plane_at(k)))

    for q, (c0, n) in enumerate(CHUNKS):
        pltpu.make_async_copy(
            slab.at[pl.ds(c0, n), :, pl.ds(pl.multiple_of(me * rows, rows), rows)],
            buf.at[me, pl.ds(c0, n)],
            recv_sem.at[q],
        ).start()

    def side(i, src, dst):
        return pltpu.make_async_remote_copy(
            src, dst, side_send.at[i], side_recv.at[i],
            device_id={"tile": tile + 1}, device_id_type=MESH,
        )

    side_fp, side_tr = side(0, fp, nb_fp), side(1, tr, nb_tr)
    side_meta = side(2, own_meta, nb_meta)
    loads[0].wait()
    loads[1].wait()
    lane = lax.broadcasted_iota(jnp.int32, (1, slots), 1)
    own_meta[...] = jnp.zeros_like(own_meta)
    own_meta[0:1, 0:slots] = own_corner[0:1, :]
    own_meta[1:2, 0:slots] = jnp.where(lane < own_count[0, 0], own_corner[1:2, :], GONE)

    @pl.when(right_second & jnp.logical_not(late))
    def _():
        pl.semaphore_wait(side_in.at[1], 1)

    @pl.when(has_right & jnp.logical_not(late))
    def _():
        side_meta.start()
        side_tr.start()
        side_fp.start()

    def send_to_later(low, high):
        @pl.loop(jnp.maximum(place + 1, low), jnp.maximum(place + 1, high))
        def _(k):
            peer = plane_at(k)
            pl.semaphore_wait(plane_in.at[peer], 1)
            for q in range(len(CHUNKS)):
                send(q, peer)

    quarter_planes = half // 2
    low_helper, high_helper = me < 2, (me >= half - 2) & (me < half)
    core = lax.rem(me, 2)

    def pass_on(helper):
        for i in range(quarter_planes // 2):

            @pl.when(helper & left_second)
            def _(i=i):
                if i == 0:
                    pl.semaphore_wait(side_in.at[0], 1)
                pl.semaphore_signal(
                    relay.at[i], inc=1, device_id={"tile": tile - 1}, device_id_type=MESH
                )

    def hand_on(helper, base):
        for i in range(quarter_planes // 2):

            @pl.when(helper & right_first)
            def _(i=i):
                pl.semaphore_wait(relay.at[i], 1)
                pl.semaphore_signal(
                    side_in.at[1], inc=1, device_id={"plane": base + 2 * i + core},
                    device_id_type=MESH,
                )

    send_to_later(0, half + quarter_planes)
    pass_on(high_helper)
    send_to_later(half + quarter_planes, n_plane)
    pass_on(low_helper)
    hand_on(high_helper, half)
    hand_on(low_helper, half + quarter_planes)

    @pl.when((right_second | right_first) & late)
    def _():
        pl.semaphore_wait(side_in.at[1], 1)

    @pl.when(right_first & late)
    def _():
        pl.semaphore_signal(side_in.at[0], inc=1, device_id={"tile": tile + 1}, device_id_type=MESH)

    @pl.when(has_right & late)
    def _():
        side_meta.start()
        side_tr.start()
        side_fp.start()

    loads[2].wait()
    loads[3].wait()

    @pl.when(has_left)
    def _():
        side_meta.wait_recv()
        side_tr.wait_recv()
        side_fp.wait_recv()

    @pl.when(jnp.logical_not(has_left))
    def _():
        nb_meta[...] = jnp.full(nb_meta.shape, GONE, jnp.int32)
        nb_tr[...] = jnp.zeros_like(nb_tr)
        nb_fp[...] = jnp.zeros_like(nb_fp)

    top = mixed_order(column_of(nb_meta[0:1, 0:slots]), column_of(own_meta[0:1, 0:slots]))
    first = mixed_order(
        column_of(nb_meta[1:2, 0:slots]) - cols, column_of(own_meta[1:2, 0:slots])
    )
    alive = first < cols
    patch[...] = mixed_order(nb_fp[...], own_fp[...])
    trace = mixed_order(nb_tr[...], own_tr[...])
    gram = lax.dot_general(
        trace, trace, (((1,), (1,)), ((), ())),
        precision=lax.Precision.HIGHEST, preferred_element_type=jnp.float32,
    )
    eye = lax.broadcasted_iota(jnp.int32, (both, both), 0) == lax.broadcasted_iota(
        jnp.int32, (both, both), 1
    )
    diagonal = jnp.sum(jnp.where(eye, gram, 0.0), axis=1, keepdims=True)
    scale = jnp.where(alive, diagonal, 1.0)
    high, low = split(jnp.where(eye, 0.0, gram) / scale)
    for g in range(GROUPS):
        at = slice(g * slots, (g + 1) * slots)
        weights[g, 0:slots, 0:both] = high[at]
        weights[g, 0:slots, both : 2 * both] = high[at]
        weights[g, slots:both, 0:both] = low[at]
        weights[g, slots:both, both : 2 * both] = jnp.zeros((slots, both), jnp.bfloat16)
    trace_bf[...] = trace.astype(jnp.bfloat16)
    inverse_at[...] = jnp.broadcast_to(1.0 / scale, (both, rows))

    i_at = lax.broadcasted_iota(jnp.int32, (both, rows), 1) - top
    row_at[...] = jnp.where((i_at >= 0) & (i_at < PR), i_at, -1)
    first_at[...] = jnp.broadcast_to(first, (both, rows))
    lane_row = lax.broadcasted_iota(jnp.int32, (both, LANES), 1)
    pick_at[...] = jnp.broadcast_to(top, (both, LANES)) + (lane_row & (PR - 1))

    def box_of(c):
        i_of = row_at[...]
        j_of = c - first_at[...]
        return i_of, j_of, (i_of >= 0) & (j_of >= 0) & (j_of < PC)

    def multiply(g, parts):
        stacked = jnp.concatenate([p[0] for p in parts] + [p[1] for p in parts], axis=0)
        product = jnp.dot(weights[g], stacked, preferred_element_type=jnp.float32)
        return product[0:slots] + product[slots:both]

    @pl.loop(0, cols // 2)
    def _(pair):
        highs, lows = [], []
        for c in (2 * pair, 2 * pair + 1):
            i_of, j_of, inside = box_of(c)
            at = (i_of & 7) * PC + (j_of & (PC - 1))
            lower = jnp.take_along_axis(patch[:, 0:LANES], at, axis=1)
            upper = jnp.take_along_axis(patch[:, LANES : 2 * LANES], at, axis=1)
            high, low = split(jnp.where(inside, jnp.where(i_of >= 8, upper, lower), 0.0))
            later_high[c] = high[slots:both]
            later_low[c] = low[slots:both]
            highs.append(high)
            lows.append(low)
        mixed = multiply(0, [(jnp.concatenate(highs, axis=1), jnp.concatenate(lows, axis=1))])
        first_mixed[2 * pair] = mixed[:, 0:rows]
        first_mixed[2 * pair + 1] = mixed[:, rows : 2 * rows]

    lane = lax.broadcasted_iota(jnp.int32, (quarter, LANES), 1)
    lane_spot = lane >> 4

    def take_back(c0, n, done, which, target):
        kept = target[c0 // BLOCK] if c0 % BLOCK else jnp.zeros((quarter, LANES), jnp.float32)
        for g in range(GROUPS):
            a = g * slots + which * quarter
            for c in range(n):
                got = jnp.take_along_axis(
                    done[a : a + quarter, c * rows : (c + 1) * rows],
                    pick_at[a : a + quarter, :],
                    axis=1,
                )
                kept = jnp.where(lane_spot == g * BLOCK + (c0 + c) % BLOCK, got, kept)
        target[c0 // BLOCK] = kept

    def back(b):
        return pltpu.make_async_remote_copy(
            left_piece.at[b], ret_piece.at[b], ret_send.at[b], ret_recv.at[b],
            device_id={"tile": tile - 1}, device_id_type=MESH,
        )

    def place_back(b, pieces, sofar):
        new = []
        for g in range(GROUPS):
            a = g * slots + quarter
            for h in range(2):
                column = first_at[a : a + quarter, :] + (lane & (PC - 1))
                at = g * (BLOCK * PR) + (column & (BLOCK - 1)) * PR + (lane >> 4) + 8 * h
                got = jnp.take_along_axis(pieces, at, axis=1)
                new.append(jnp.where((column >> 2) == b, got, sofar[g * 2 + h]))
        return new

    n_block = cols // BLOCK
    boxes = [jnp.zeros((quarter, LANES), jnp.float32)] * (2 * GROUPS)
    for c0 in range(0, cols, BLOCK):
        n = BLOCK
        for q, (start, width) in enumerate(CHUNKS):
            if start == c0:
                landed = buf.at[:, pl.ds(start, width)]
                pltpu.make_async_copy(landed, landed, recv_sem.at[q]).wait()
        data, signal = [], []
        for c in range(c0, c0 + n):
            block = buf[:, c].astype(jnp.float32)
            data.append(block.reshape(-1, rows).astype(jnp.bfloat16))
        summed = jnp.dot(
            trace_bf[...], jnp.concatenate(data, axis=1), preferred_element_type=jnp.float32
        )
        for c in range(n):
            _, _, inside = box_of(c0 + c)
            signal.append(
                jnp.where(inside, summed[:, c * rows : (c + 1) * rows] * inverse_at[...], -jnp.inf)
            )
        signal = jnp.concatenate(signal, axis=1)
        signal = [signal[g * slots : (g + 1) * slots] for g in range(GROUPS)]
        wide = lambda ref: jnp.concatenate([ref[c] for c in range(c0, c0 + n)], axis=1)
        now = [None] * GROUPS
        parts = [None] + [(wide(later_high), wide(later_low))]
        mixed = wide(first_mixed)
        for step in range(SWEEPS * GROUPS):
            g = step % GROUPS
            if step > 0:
                mixed = multiply(g, parts)
            now[g] = jnp.maximum(signal[g] - mixed, 0.0)
            parts[g] = split(now[g])
        done = jnp.concatenate(now, axis=0)
        if True:
            take_back(c0, n, done, 0, left_piece)
        if c0 == 0:

            @pl.when(left_second & jnp.logical_not(low_helper | high_helper))
            def _():
                pl.semaphore_wait(side_in.at[0], 1)

        if (c0 + n) % BLOCK == 0:

            @pl.when(has_left)
            def _(b=c0 // BLOCK):
                back(b).start()

        take_back(c0, n, done, 1, own_piece)
        if (c0 + n) % BLOCK == 0:
            boxes = place_back(c0 // BLOCK, own_piece[c0 // BLOCK], boxes)

    @pl.when(has_right)
    def _():
        for copy in (side_fp, side_tr, side_meta):
            copy.wait_send()

    @pl.when(jnp.logical_not(has_right))
    def _():
        ret_piece[...] = jnp.zeros_like(ret_piece)

    for b in range(n_block):

        @pl.when(has_right)
        def _(b=b):
            back(b).wait_recv()

        boxes = place_back(n_block + b, ret_piece[b], boxes)
    for g in range(GROUPS):
        for h in range(2):
            out[g * quarter : (g + 1) * quarter, h * LANES : (h + 1) * LANES] = boxes[g * 2 + h]

    for q, (c0, n) in enumerate(CHUNKS):
        gone_out = buf.at[pl.ds(0, n_plane - 1), pl.ds(c0, n)]
        pltpu.make_async_copy(gone_out, gone_out, send_sem.at[q]).wait()

    @pl.when(has_left)
    def _():
        for b in range(n_block):
            back(b).wait_send()


def body(slab_data, footprints, traces, corners, counts):
    n_tile, n_plane = lax.axis_size("tile"), lax.axis_size("plane")
    cols, frames, rows = slab_data.shape
    rows = rows // n_plane
    slots, box = footprints.shape
    span = traces.shape[1]
    both = 2 * slots
    hbm = pl.BlockSpec(memory_space=pltpu.HBM)
    vmem = pl.BlockSpec(memory_space=pltpu.VMEM)
    f32, bf16, i32 = jnp.float32, jnp.bfloat16, jnp.int32
    dma = pltpu.SemaphoreType.DMA
    regular = pltpu.SemaphoreType.REGULAR
    return pl.pallas_call(
        functools.partial(kernel, n_tile, n_plane),
        out_shape=pltpu.VMEM((slots, box), f32),
        in_specs=[hbm] * 5,
        out_specs=vmem,
        scratch_shapes=[
            pltpu.VMEM((n_plane, cols, frames, rows), bf16),
            pltpu.VMEM((slots, box), f32),
            pltpu.VMEM((slots, box), f32),
            pltpu.VMEM((slots, span), f32),
            pltpu.VMEM((slots, span), f32),
            pltpu.VMEM((2, slots), i32),
            pltpu.VMEM((8, 128), i32),
            pltpu.VMEM((8, 128), i32),
            pltpu.SMEM((1, 1), i32),
            pltpu.VMEM((both, box), f32),
            pltpu.VMEM((cols, slots, rows), f32),
            pltpu.VMEM((cols, slots, rows), bf16),
            pltpu.VMEM((cols, slots, rows), bf16),
            pltpu.VMEM((both, rows), i32),
            pltpu.VMEM((both, rows), i32),
            pltpu.VMEM((both, LANES), i32),
            pltpu.VMEM((both, rows), f32),
            pltpu.VMEM((GROUPS, both, 2 * both), bf16),
            pltpu.VMEM((both, span), bf16),
            pltpu.VMEM((cols // BLOCK, slots // GROUPS, LANES), f32),
            pltpu.VMEM((cols // BLOCK, slots // GROUPS, LANES), f32),
            pltpu.VMEM((cols // BLOCK, slots // GROUPS, LANES), f32),
            dma((4,)),
            dma((len(CHUNKS),)),
            dma((len(CHUNKS),)),
            dma((3,)),
            dma((3,)),
            dma((cols // BLOCK,)),
            dma((cols // BLOCK,)),
            regular((n_plane,)),
            regular((2,)),
            regular((n_plane // 8,)),
        ],
        compiler_params=pltpu.CompilerParams(
            collective_id=0, has_side_effects=True, vmem_limit_bytes=60 << 20
        ),
    )(slab_data, footprints, traces, corners.T, counts.reshape(1, 1))


def solution(mesh):
    in_specs = (
        P("tile", "plane", None),
        P(("tile", "plane"), None),
        P(("tile", "plane"), None),
        P(("tile", "plane"), None),
        P(("tile", "plane")),
    )
    out_specs = P(("tile", "plane"), None)
    return jax.shard_map(body, mesh=mesh, in_specs=in_specs, out_specs=out_specs, check_vma=False)
```

```python
import functools

import jax
import jax.numpy as jnp
from jax import lax
from jax.experimental import pallas as pl
from jax.experimental.pallas import tpu as pltpu
from jax.sharding import PartitionSpec as P

PR = 16
PC = 16
SWEEPS = 2
GROUPS = 2
CHUNKS = ((0, 8), (8, 4), (12, 4))
BLOCK = 4
X_SIZE = 4
LANES = 128
MESH = pl.DeviceIdType.MESH
GONE = 1 << 14


def mixed_order(left, own):
    half = own.shape[0] // GROUPS
    parts = []
    for g in range(GROUPS):
        parts += [left[g * half : (g + 1) * half], own[g * half : (g + 1) * half]]
    return jnp.concatenate(parts, axis=0)


def column_of(row):
    n = row.shape[1]
    eye = lax.broadcasted_iota(jnp.int32, (n, n), 0) == lax.broadcasted_iota(jnp.int32, (n, n), 1)
    spread = jnp.where(eye, jnp.broadcast_to(row.astype(jnp.float32), (n, n)), 0.0)
    return jnp.sum(spread, axis=1, keepdims=True).astype(jnp.int32)


def split(x):
    high = x.astype(jnp.bfloat16)
    return high, (x - high.astype(jnp.float32)).astype(jnp.bfloat16)


def kernel(
    n_tile, n_plane, slab, fp, tr, corners, counts, out,
    buf, own_fp, nb_fp, own_tr, nb_tr, own_corner, own_meta, nb_meta, own_count,
    patch, first_mixed, later_high, later_low, row_at, first_at, pick_at, inverse_at,
    weights, trace_bf, left_piece, ret_piece,
    load_sem, send_sem, recv_sem, side_send, side_recv, ret_send, ret_recv, plane_in, side_in, relay,
):
    cols, rows = buf.shape[1], buf.shape[3]
    slots = own_fp.shape[0]
    both = 2 * slots
    quarter = slots // GROUPS
    tile, me = lax.axis_index("tile"), lax.axis_index("plane")
    has_left, has_right = tile > 0, tile < n_tile - 1
    half = n_plane // 2
    place = jnp.where(me == 0, half - 1, jnp.where(me < half, me - 1, me))

    late = place >= half

    def plane_at(k):
        return jnp.where(k < half - 1, k + 1, jnp.where(k == half - 1, 0, k))

    left_first = has_left & (lax.rem(tile, X_SIZE) != 0)
    left_second = has_left & (lax.rem(tile, X_SIZE) == 0)
    right_second = has_right & (lax.rem(tile + 1, X_SIZE) != 0)
    right_first = has_right & (lax.rem(tile + 1, X_SIZE) == 0)

    barrier = pltpu.get_barrier_semaphore()

    @pl.loop(place + 1, n_plane)
    def _(k):
        pl.semaphore_signal(
            barrier, inc=1, device_id={"plane": plane_at(k)}, device_id_type=MESH
        )

    @pl.when(right_second)
    def _():
        pl.semaphore_signal(barrier, inc=1, device_id={"tile": tile + 1}, device_id_type=MESH)

    @pl.when(left_second & jnp.logical_not(late))
    def _():
        pl.semaphore_signal(barrier, inc=1, device_id={"tile": tile - 1}, device_id_type=MESH)

    loads = [
        pltpu.make_async_copy(src, dst, load_sem.at[i])
        for i, (src, dst) in enumerate(
            ((corners, own_corner), (counts, own_count), (tr, own_tr), (fp, own_fp))
        )
    ]
    for load in loads:
        load.start()
    right_told = right_first & jnp.logical_not(late)
    before = place + left_first.astype(jnp.int32) + right_told.astype(jnp.int32)

    @pl.when(before > 0)
    def _():
        pl.semaphore_wait(barrier, before)

    @pl.loop(0, place)
    def _(k):
        pl.semaphore_signal(
            plane_in.at[me], inc=1, device_id={"plane": plane_at(k)}, device_id_type=MESH
        )

    @pl.when(left_first)
    def _():
        pl.semaphore_signal(side_in.at[1], inc=1, device_id={"tile": tile - 1}, device_id_type=MESH)

    @pl.when(right_told)
    def _():
        pl.semaphore_signal(side_in.at[0], inc=1, device_id={"tile": tile + 1}, device_id_type=MESH)

    def send(q, peer):
        c0, n = CHUNKS[q]
        pltpu.make_async_remote_copy(
            slab.at[pl.ds(c0, n), :, pl.ds(pl.multiple_of(peer * rows, rows), rows)],
            buf.at[me, pl.ds(c0, n)],
            send_sem.at[q],
            recv_sem.at[q],
            device_id={"plane": peer},
            device_id_type=MESH,
        ).start()

    early = jnp.minimum(place, half)
    for a, b in ((0, 2), (2, half), (half, n_plane)):
        for q in range(len(CHUNKS)):

            @pl.loop(jnp.minimum(a, place), jnp.minimum(b, place))
            def _(k, q=q):
                send(q, jnp.where(late, k, plane_at(k)))

    for q, (c0, n) in enumerate(CHUNKS):
        pltpu.make_async_copy(
            slab.at[pl.ds(c0, n), :, pl.ds(pl.multiple_of(me * rows, rows), rows)],
            buf.at[me, pl.ds(c0, n)],
            recv_sem.at[q],
        ).start()

    def side(i, src, dst):
        return pltpu.make_async_remote_copy(
            src, dst, side_send.at[i], side_recv.at[i],
            device_id={"tile": tile + 1}, device_id_type=MESH,
        )

    side_fp, side_tr = side(0, fp, nb_fp), side(1, tr, nb_tr)
    side_meta = side(2, own_meta, nb_meta)
    loads[0].wait()
    loads[1].wait()
    lane = lax.broadcasted_iota(jnp.int32, (1, slots), 1)
    own_meta[...] = jnp.zeros_like(own_meta)
    own_meta[0:1, 0:slots] = own_corner[0:1, :]
    own_meta[1:2, 0:slots] = jnp.where(lane < own_count[0, 0], own_corner[1:2, :], GONE)

    @pl.when(right_second & jnp.logical_not(late))
    def _():
        pl.semaphore_wait(side_in.at[1], 1)

    @pl.when(has_right & jnp.logical_not(late))
    def _():
        side_meta.start()
        side_tr.start()
        side_fp.start()

    def send_to_later(low, high):
        @pl.loop(jnp.maximum(place + 1, low), jnp.maximum(place + 1, high))
        def _(k):
            peer = plane_at(k)
            pl.semaphore_wait(plane_in.at[peer], 1)
            for q in range(len(CHUNKS)):
                send(q, peer)

    quarter_planes = half // 2
    low_helper, high_helper = me < 2, (me >= half - 2) & (me < half)
    core = lax.rem(me, 2)

    def pass_on(helper):
        for i in range(quarter_planes // 2):

            @pl.when(helper & left_second)
            def _(i=i):
                if i == 0:
                    pl.semaphore_wait(side_in.at[0], 1)
                pl.semaphore_signal(
                    relay.at[i], inc=1, device_id={"tile": tile - 1}, device_id_type=MESH
                )

    def hand_on(helper, base):
        for i in range(quarter_planes // 2):

            @pl.when(helper & right_first)
            def _(i=i):
                pl.semaphore_wait(relay.at[i], 1)
                pl.semaphore_signal(
                    side_in.at[1], inc=1, device_id={"plane": base + 2 * i + core},
                    device_id_type=MESH,
                )

    send_to_later(0, half + quarter_planes)
    pass_on(high_helper)
    send_to_later(half + quarter_planes, n_plane)
    pass_on(low_helper)
    hand_on(high_helper, half)
    hand_on(low_helper, half + quarter_planes)

    @pl.when((right_second | right_first) & late)
    def _():
        pl.semaphore_wait(side_in.at[1], 1)

    @pl.when(right_first & late)
    def _():
        pl.semaphore_signal(side_in.at[0], inc=1, device_id={"tile": tile + 1}, device_id_type=MESH)

    @pl.when(has_right & late)
    def _():
        side_meta.start()
        side_tr.start()
        side_fp.start()

    loads[2].wait()
    loads[3].wait()

    @pl.when(has_left)
    def _():
        side_meta.wait_recv()
        side_tr.wait_recv()
        side_fp.wait_recv()

    @pl.when(jnp.logical_not(has_left))
    def _():
        nb_meta[...] = jnp.full(nb_meta.shape, GONE, jnp.int32)
        nb_tr[...] = jnp.zeros_like(nb_tr)
        nb_fp[...] = jnp.zeros_like(nb_fp)

    top = mixed_order(column_of(nb_meta[0:1, 0:slots]), column_of(own_meta[0:1, 0:slots]))
    first = mixed_order(
        column_of(nb_meta[1:2, 0:slots]) - cols, column_of(own_meta[1:2, 0:slots])
    )
    alive = first < cols
    patch[...] = mixed_order(nb_fp[...], own_fp[...])
    trace = mixed_order(nb_tr[...], own_tr[...])
    gram = lax.dot_general(
        trace, trace, (((1,), (1,)), ((), ())),
        precision=lax.Precision.HIGHEST, preferred_element_type=jnp.float32,
    )
    eye = lax.broadcasted_iota(jnp.int32, (both, both), 0) == lax.broadcasted_iota(
        jnp.int32, (both, both), 1
    )
    diagonal = jnp.sum(jnp.where(eye, gram, 0.0), axis=1, keepdims=True)
    scale = jnp.where(alive, diagonal, 1.0)
    high, low = split(jnp.where(eye, 0.0, gram) / scale)
    for g in range(GROUPS):
        at = slice(g * slots, (g + 1) * slots)
        weights[g, 0:slots, 0:both] = high[at]
        weights[g, 0:slots, both : 2 * both] = high[at]
        weights[g, slots:both, 0:both] = low[at]
        weights[g, slots:both, both : 2 * both] = jnp.zeros((slots, both), jnp.bfloat16)
    trace_bf[...] = trace.astype(jnp.bfloat16)
    inverse_at[...] = jnp.broadcast_to(1.0 / scale, (both, rows))

    i_at = lax.broadcasted_iota(jnp.int32, (both, rows), 1) - top
    row_at[...] = jnp.where((i_at >= 0) & (i_at < PR), i_at, -1)
    first_at[...] = jnp.broadcast_to(first, (both, rows))
    lane_row = lax.broadcasted_iota(jnp.int32, (both, LANES), 1)
    pick_at[...] = jnp.broadcast_to(top, (both, LANES)) + (lane_row & (PR - 1))

    def box_of(c):
        i_of = row_at[...]
        j_of = c - first_at[...]
        return i_of, j_of, (i_of >= 0) & (j_of >= 0) & (j_of < PC)

    def multiply(g, parts):
        stacked = jnp.concatenate([p[0] for p in parts] + [p[1] for p in parts], axis=0)
        product = jnp.dot(weights[g], stacked, preferred_element_type=jnp.float32)
        return product[0:slots] + product[slots:both]

    @pl.loop(0, cols // 2)
    def _(pair):
        highs, lows = [], []
        for c in (2 * pair, 2 * pair + 1):
            i_of, j_of, inside = box_of(c)
            at = (i_of & 7) * PC + (j_of & (PC - 1))
            lower = jnp.take_along_axis(patch[:, 0:LANES], at, axis=1)
            upper = jnp.take_along_axis(patch[:, LANES : 2 * LANES], at, axis=1)
            high, low = split(jnp.where(inside, jnp.where(i_of >= 8, upper, lower), 0.0))
            later_high[c] = high[slots:both]
            later_low[c] = low[slots:both]
            highs.append(high)
            lows.append(low)
        mixed = multiply(0, [(jnp.concatenate(highs, axis=1), jnp.concatenate(lows, axis=1))])
        first_mixed[2 * pair] = mixed[:, 0:rows]
        first_mixed[2 * pair + 1] = mixed[:, rows : 2 * rows]

    lane = lax.broadcasted_iota(jnp.int32, (quarter, LANES), 1)
    lane_spot = lane >> 4

    def take_back(done, which):
        kept = jnp.zeros((quarter, LANES), jnp.float32)
        for g in range(GROUPS):
            a = g * slots + which * quarter
            for c in range(BLOCK):
                got = jnp.take_along_axis(
                    done[a : a + quarter, c * rows : (c + 1) * rows],
                    pick_at[a : a + quarter, :],
                    axis=1,
                )
                kept = jnp.where(lane_spot == g * BLOCK + c, got, kept)
        return kept

    def back(b):
        return pltpu.make_async_remote_copy(
            left_piece.at[b], ret_piece.at[b], ret_send.at[b], ret_recv.at[b],
            device_id={"tile": tile - 1}, device_id_type=MESH,
        )

    def place_back(b, pieces):
        for g in range(GROUPS):
            a = g * slots + quarter
            for h in range(2):
                column = first_at[a : a + quarter, :] + (lane & (PC - 1))
                at = g * (BLOCK * PR) + (column & (BLOCK - 1)) * PR + (lane >> 4) + 8 * h
                got = jnp.take_along_axis(pieces, at, axis=1)
                where = (slice(g * quarter, (g + 1) * quarter), slice(h * LANES, (h + 1) * LANES))
                out[where] = jnp.where((column >> 2) == b, got, out[where])

    n_block = cols // BLOCK
    out[...] = jnp.zeros_like(out)

    @pl.when(left_second & jnp.logical_not(low_helper | high_helper))
    def _():
        pl.semaphore_wait(side_in.at[0], 1)

    @pl.loop(0, n_block)
    def _(b):
        for q, (start, width) in enumerate(CHUNKS):

            @pl.when(b * BLOCK == start)
            def _(q=q, start=start, width=width):
                landed = buf.at[:, pl.ds(start, width)]
                pltpu.make_async_copy(landed, landed, recv_sem.at[q]).wait()

        columns = [b * BLOCK + c for c in range(BLOCK)]
        data, signal = [], []
        for c in columns:
            block = buf[:, c].astype(jnp.float32)
            data.append(block.reshape(-1, rows).astype(jnp.bfloat16))
        summed = jnp.dot(
            trace_bf[...], jnp.concatenate(data, axis=1), preferred_element_type=jnp.float32
        )
        for i, c in enumerate(columns):
            _, _, inside = box_of(c)
            signal.append(
                jnp.where(inside, summed[:, i * rows : (i + 1) * rows] * inverse_at[...], -jnp.inf)
            )
        signal = jnp.concatenate(signal, axis=1)
        signal = [signal[g * slots : (g + 1) * slots] for g in range(GROUPS)]
        wide = lambda ref: jnp.concatenate([ref[c] for c in columns], axis=1)
        now = [None] * GROUPS
        parts = [None, (wide(later_high), wide(later_low))]
        mixed = wide(first_mixed)
        for step in range(SWEEPS * GROUPS):
            g = step % GROUPS
            if step > 0:
                mixed = multiply(g, parts)
            now[g] = jnp.maximum(signal[g] - mixed, 0.0)
            parts[g] = split(now[g])
        done = jnp.concatenate(now, axis=0)
        left_piece[b] = take_back(done, 0)

        @pl.when(has_left)
        def _():
            back(b).start()

        place_back(b, take_back(done, 1))

    @pl.when(has_right)
    def _():
        for copy in (side_fp, side_tr, side_meta):
            copy.wait_send()

    @pl.when(jnp.logical_not(has_right))
    def _():
        ret_piece[...] = jnp.zeros_like(ret_piece)

    @pl.loop(0, n_block)
    def _(b):
        @pl.when(has_right)
        def _():
            back(b).wait_recv()

        place_back(n_block + b, ret_piece[b])

    for q, (c0, n) in enumerate(CHUNKS):
        gone_out = buf.at[pl.ds(0, n_plane - 1), pl.ds(c0, n)]
        pltpu.make_async_copy(gone_out, gone_out, send_sem.at[q]).wait()

    @pl.when(has_left)
    def _():
        for b in range(n_block):
            back(b).wait_send()


def body(slab_data, footprints, traces, corners, counts):
    n_tile, n_plane = lax.axis_size("tile"), lax.axis_size("plane")
    cols, frames, rows = slab_data.shape
    rows = rows // n_plane
    slots, box = footprints.shape
    span = traces.shape[1]
    both = 2 * slots
    hbm = pl.BlockSpec(memory_space=pltpu.HBM)
    vmem = pl.BlockSpec(memory_space=pltpu.VMEM)
    f32, bf16, i32 = jnp.float32, jnp.bfloat16, jnp.int32
    dma = pltpu.SemaphoreType.DMA
    regular = pltpu.SemaphoreType.REGULAR
    return pl.pallas_call(
        functools.partial(kernel, n_tile, n_plane),
        out_shape=pltpu.VMEM((slots, box), f32),
        in_specs=[hbm] * 5,
        out_specs=vmem,
        scratch_shapes=[
            pltpu.VMEM((n_plane, cols, frames, rows), bf16),
            pltpu.VMEM((slots, box), f32),
            pltpu.VMEM((slots, box), f32),
            pltpu.VMEM((slots, span), f32),
            pltpu.VMEM((slots, span), f32),
            pltpu.VMEM((2, slots), i32),
            pltpu.VMEM((8, 128), i32),
            pltpu.VMEM((8, 128), i32),
            pltpu.SMEM((1, 1), i32),
            pltpu.VMEM((both, box), f32),
            pltpu.VMEM((cols, slots, rows), f32),
            pltpu.VMEM((cols, slots, rows), bf16),
            pltpu.VMEM((cols, slots, rows), bf16),
            pltpu.VMEM((both, rows), i32),
            pltpu.VMEM((both, rows), i32),
            pltpu.VMEM((both, LANES), i32),
            pltpu.VMEM((both, rows), f32),
            pltpu.VMEM((GROUPS, both, 2 * both), bf16),
            pltpu.VMEM((both, span), bf16),
            pltpu.VMEM((cols // BLOCK, slots // GROUPS, LANES), f32),
            pltpu.VMEM((cols // BLOCK, slots // GROUPS, LANES), f32),
            dma((4,)),
            dma((len(CHUNKS),)),
            dma((len(CHUNKS),)),
            dma((3,)),
            dma((3,)),
            dma((cols // BLOCK,)),
            dma((cols // BLOCK,)),
            regular((n_plane,)),
            regular((2,)),
            regular((n_plane // 8,)),
        ],
        compiler_params=pltpu.CompilerParams(
            collective_id=0, has_side_effects=True, vmem_limit_bytes=60 << 20
        ),
    )(slab_data, footprints, traces, corners.T, counts.reshape(1, 1))


def solution(mesh):
    in_specs = (
        P("tile", "plane", None),
        P(("tile", "plane"), None),
        P(("tile", "plane"), None),
        P(("tile", "plane"), None),
        P(("tile", "plane")),
    )
    out_specs = P(("tile", "plane"), None)
    return jax.shard_map(body, mesh=mesh, in_specs=in_specs, out_specs=out_specs, check_vma=False)
```

```python
import functools

import jax
import jax.numpy as jnp
from jax import lax
from jax.experimental import pallas as pl
from jax.experimental.pallas import tpu as pltpu
from jax.sharding import PartitionSpec as P

PR = 16
PC = 16
SWEEPS = 2
GROUPS = 2
CHUNKS = ((0, 8), (8, 4), (12, 4))
BLOCK = 4
X_SIZE = 4
LANES = 128
MESH = pl.DeviceIdType.MESH
GONE = 1 << 14


def mixed_order(left, own):
    half = own.shape[0] // GROUPS
    parts = []
    for g in range(GROUPS):
        parts += [left[g * half : (g + 1) * half], own[g * half : (g + 1) * half]]
    return jnp.concatenate(parts, axis=0)


def column_of(row):
    n = row.shape[1]
    eye = lax.broadcasted_iota(jnp.int32, (n, n), 0) == lax.broadcasted_iota(jnp.int32, (n, n), 1)
    spread = jnp.where(eye, jnp.broadcast_to(row.astype(jnp.float32), (n, n)), 0.0)
    return jnp.sum(spread, axis=1, keepdims=True).astype(jnp.int32)


def split(x):
    high = x.astype(jnp.bfloat16)
    return high, (x - high.astype(jnp.float32)).astype(jnp.bfloat16)


def kernel(
    n_tile, n_plane, slab, fp, tr, corners, counts, out,
    buf, own_fp, nb_fp, own_tr, nb_tr, own_corner, own_meta, nb_meta, own_count,
    patch, first_mixed, later_high, later_low, row_at, first_at, pick_at, inverse_at,
    weights, half_weights, trace_bf, left_piece, ret_piece,
    load_sem, send_sem, recv_sem, side_send, side_recv, ret_send, ret_recv, plane_in, side_in, relay,
):
    cols, rows = buf.shape[1], buf.shape[3]
    slots = own_fp.shape[0]
    both = 2 * slots
    quarter = slots // GROUPS
    tile, me = lax.axis_index("tile"), lax.axis_index("plane")
    has_left, has_right = tile > 0, tile < n_tile - 1
    half = n_plane // 2
    place = jnp.where(me == 0, half - 1, jnp.where(me < half, me - 1, me))

    late = place >= half

    def plane_at(k):
        return jnp.where(k < half - 1, k + 1, jnp.where(k == half - 1, 0, k))

    left_first = has_left & (lax.rem(tile, X_SIZE) != 0)
    left_second = has_left & (lax.rem(tile, X_SIZE) == 0)
    right_second = has_right & (lax.rem(tile + 1, X_SIZE) != 0)
    right_first = has_right & (lax.rem(tile + 1, X_SIZE) == 0)

    barrier = pltpu.get_barrier_semaphore()

    @pl.loop(place + 1, n_plane)
    def _(k):
        pl.semaphore_signal(
            barrier, inc=1, device_id={"plane": plane_at(k)}, device_id_type=MESH
        )

    @pl.when(right_second)
    def _():
        pl.semaphore_signal(barrier, inc=1, device_id={"tile": tile + 1}, device_id_type=MESH)

    @pl.when(left_second & jnp.logical_not(late))
    def _():
        pl.semaphore_signal(barrier, inc=1, device_id={"tile": tile - 1}, device_id_type=MESH)

    loads = [
        pltpu.make_async_copy(src, dst, load_sem.at[i])
        for i, (src, dst) in enumerate(
            ((corners, own_corner), (counts, own_count), (tr, own_tr), (fp, own_fp))
        )
    ]
    for load in loads:
        load.start()
    right_told = right_first & jnp.logical_not(late)
    before = place + left_first.astype(jnp.int32) + right_told.astype(jnp.int32)

    @pl.when(before > 0)
    def _():
        pl.semaphore_wait(barrier, before)

    @pl.loop(0, place)
    def _(k):
        pl.semaphore_signal(
            plane_in.at[me], inc=1, device_id={"plane": plane_at(k)}, device_id_type=MESH
        )

    @pl.when(left_first)
    def _():
        pl.semaphore_signal(side_in.at[1], inc=1, device_id={"tile": tile - 1}, device_id_type=MESH)

    @pl.when(right_told)
    def _():
        pl.semaphore_signal(side_in.at[0], inc=1, device_id={"tile": tile + 1}, device_id_type=MESH)

    def send(q, peer):
        c0, n = CHUNKS[q]
        pltpu.make_async_remote_copy(
            slab.at[pl.ds(c0, n), :, pl.ds(pl.multiple_of(peer * rows, rows), rows)],
            buf.at[me, pl.ds(c0, n)],
            send_sem.at[q],
            recv_sem.at[q],
            device_id={"plane": peer},
            device_id_type=MESH,
        ).start()

    early = jnp.minimum(place, half)
    for a, b in ((0, 2), (2, half), (half, n_plane)):
        for q in range(len(CHUNKS)):

            @pl.loop(jnp.minimum(a, place), jnp.minimum(b, place))
            def _(k, q=q):
                send(q, jnp.where(late, k, plane_at(k)))

    for q, (c0, n) in enumerate(CHUNKS):
        pltpu.make_async_copy(
            slab.at[pl.ds(c0, n), :, pl.ds(pl.multiple_of(me * rows, rows), rows)],
            buf.at[me, pl.ds(c0, n)],
            recv_sem.at[q],
        ).start()

    def side(i, src, dst):
        return pltpu.make_async_remote_copy(
            src, dst, side_send.at[i], side_recv.at[i],
            device_id={"tile": tile + 1}, device_id_type=MESH,
        )

    side_fp, side_tr = side(0, fp, nb_fp), side(1, tr, nb_tr)
    side_meta = side(2, own_meta, nb_meta)
    loads[0].wait()
    loads[1].wait()
    lane = lax.broadcasted_iota(jnp.int32, (1, slots), 1)
    own_meta[...] = jnp.zeros_like(own_meta)
    own_meta[0:1, 0:slots] = own_corner[0:1, :]
    own_meta[1:2, 0:slots] = jnp.where(lane < own_count[0, 0], own_corner[1:2, :], GONE)

    @pl.when(right_second & jnp.logical_not(late))
    def _():
        pl.semaphore_wait(side_in.at[1], 1)

    @pl.when(has_right & jnp.logical_not(late))
    def _():
        side_meta.start()
        side_tr.start()
        side_fp.start()

    def send_to_later(low, high):
        @pl.loop(jnp.maximum(place + 1, low), jnp.maximum(place + 1, high))
        def _(k):
            peer = plane_at(k)
            pl.semaphore_wait(plane_in.at[peer], 1)
            for q in range(len(CHUNKS)):
                send(q, peer)

    quarter_planes = half // 2
    low_helper, high_helper = me < 2, (me >= half - 2) & (me < half)
    core = lax.rem(me, 2)

    def pass_on(helper):
        for i in range(quarter_planes // 2):

            @pl.when(helper & left_second)
            def _(i=i):
                if i == 0:
                    pl.semaphore_wait(side_in.at[0], 1)
                pl.semaphore_signal(
                    relay.at[i], inc=1, device_id={"tile": tile - 1}, device_id_type=MESH
                )

    def hand_on(helper, base):
        for i in range(quarter_planes // 2):

            @pl.when(helper & right_first)
            def _(i=i):
                pl.semaphore_wait(relay.at[i], 1)
                pl.semaphore_signal(
                    side_in.at[1], inc=1, device_id={"plane": base + 2 * i + core},
                    device_id_type=MESH,
                )

    send_to_later(0, half + quarter_planes)
    pass_on(high_helper)
    send_to_later(half + quarter_planes, n_plane)
    pass_on(low_helper)
    hand_on(high_helper, half)
    hand_on(low_helper, half + quarter_planes)

    @pl.when((right_second | right_first) & late)
    def _():
        pl.semaphore_wait(side_in.at[1], 1)

    @pl.when(right_first & late)
    def _():
        pl.semaphore_signal(side_in.at[0], inc=1, device_id={"tile": tile + 1}, device_id_type=MESH)

    @pl.when(has_right & late)
    def _():
        side_meta.start()
        side_tr.start()
        side_fp.start()

    loads[2].wait()
    loads[3].wait()

    @pl.when(has_left)
    def _():
        side_meta.wait_recv()
        side_tr.wait_recv()
        side_fp.wait_recv()

    @pl.when(jnp.logical_not(has_left))
    def _():
        nb_meta[...] = jnp.full(nb_meta.shape, GONE, jnp.int32)
        nb_tr[...] = jnp.zeros_like(nb_tr)
        nb_fp[...] = jnp.zeros_like(nb_fp)

    top = mixed_order(column_of(nb_meta[0:1, 0:slots]), column_of(own_meta[0:1, 0:slots]))
    first = mixed_order(
        column_of(nb_meta[1:2, 0:slots]) - cols, column_of(own_meta[1:2, 0:slots])
    )
    alive = first < cols
    patch[...] = mixed_order(nb_fp[...], own_fp[...])
    trace = mixed_order(nb_tr[...], own_tr[...])
    gram = lax.dot_general(
        trace, trace, (((1,), (1,)), ((), ())),
        precision=lax.Precision.HIGHEST, preferred_element_type=jnp.float32,
    )
    eye = lax.broadcasted_iota(jnp.int32, (both, both), 0) == lax.broadcasted_iota(
        jnp.int32, (both, both), 1
    )
    diagonal = jnp.sum(jnp.where(eye, gram, 0.0), axis=1, keepdims=True)
    scale = jnp.where(alive, diagonal, 1.0)
    high, low = split(jnp.where(eye, 0.0, gram) / scale)
    for g in range(GROUPS):
        at = slice(g * slots, (g + 1) * slots)
        weights[g, 0:slots, 0:both] = high[at]
        weights[g, 0:slots, both : 2 * both] = high[at]
        weights[g, slots:both, 0:both] = low[at]
        weights[g, slots:both, both : 2 * both] = jnp.zeros((slots, both), jnp.bfloat16)
        for of in range(GROUPS):
            src = slice(of * slots, (of + 1) * slots)
            a = of * both
            half_weights[g, 0:slots, a : a + slots] = high[at, src]
            half_weights[g, 0:slots, a + slots : a + both] = high[at, src]
            half_weights[g, slots:both, a : a + slots] = low[at, src]
            half_weights[g, slots:both, a + slots : a + both] = jnp.zeros(
                (slots, slots), jnp.bfloat16
            )
    trace_bf[...] = trace.astype(jnp.bfloat16)
    inverse_at[...] = jnp.broadcast_to(1.0 / scale, (both, rows))

    i_at = lax.broadcasted_iota(jnp.int32, (both, rows), 1) - top
    row_at[...] = jnp.where((i_at >= 0) & (i_at < PR), i_at, -1)
    first_at[...] = jnp.broadcast_to(first, (both, rows))
    lane_row = lax.broadcasted_iota(jnp.int32, (both, LANES), 1)
    pick_at[...] = jnp.broadcast_to(top, (both, LANES)) + (lane_row & (PR - 1))

    def box_of(c):
        i_of = row_at[...]
        j_of = c - first_at[...]
        return i_of, j_of, (i_of >= 0) & (j_of >= 0) & (j_of < PC)

    def multiply(g, parts):
        stacked = jnp.concatenate([p[0] for p in parts] + [p[1] for p in parts], axis=0)
        product = jnp.dot(weights[g], stacked, preferred_element_type=jnp.float32)
        return product[0:slots] + product[slots:both]

    def multiply_part(g, of, part):
        at = of * both
        stacked = jnp.concatenate(part, axis=0)
        product = jnp.dot(
            half_weights[g, :, at : at + both], stacked, preferred_element_type=jnp.float32
        )
        return product[0:slots] + product[slots:both]

    @pl.loop(0, cols // 2)
    def _(pair):
        highs, lows = [], []
        for c in (2 * pair, 2 * pair + 1):
            i_of, j_of, inside = box_of(c)
            at = (i_of & 7) * PC + (j_of & (PC - 1))
            lower = jnp.take_along_axis(patch[:, 0:LANES], at, axis=1)
            upper = jnp.take_along_axis(patch[:, LANES : 2 * LANES], at, axis=1)
            high, low = split(jnp.where(inside, jnp.where(i_of >= 8, upper, lower), 0.0))
            later_high[c] = high[slots:both]
            later_low[c] = low[slots:both]
            highs.append(high)
            lows.append(low)
        mixed = multiply(0, [(jnp.concatenate(highs, axis=1), jnp.concatenate(lows, axis=1))])
        first_mixed[2 * pair] = mixed[:, 0:rows]
        first_mixed[2 * pair + 1] = mixed[:, rows : 2 * rows]

    lane = lax.broadcasted_iota(jnp.int32, (quarter, LANES), 1)
    lane_spot = lane >> 4

    def take_back(done, which):
        kept = jnp.zeros((quarter, LANES), jnp.float32)
        for g in range(GROUPS):
            a = g * slots + which * quarter
            for c in range(BLOCK):
                got = jnp.take_along_axis(
                    done[a : a + quarter, c * rows : (c + 1) * rows],
                    pick_at[a : a + quarter, :],
                    axis=1,
                )
                kept = jnp.where(lane_spot == g * BLOCK + c, got, kept)
        return kept

    def back(b):
        return pltpu.make_async_remote_copy(
            left_piece.at[b], ret_piece.at[b], ret_send.at[b], ret_recv.at[b],
            device_id={"tile": tile - 1}, device_id_type=MESH,
        )

    def place_back(b, pieces):
        for g in range(GROUPS):
            a = g * slots + quarter
            for h in range(2):
                column = first_at[a : a + quarter, :] + (lane & (PC - 1))
                at = g * (BLOCK * PR) + (column & (BLOCK - 1)) * PR + (lane >> 4) + 8 * h
                got = jnp.take_along_axis(pieces, at, axis=1)
                where = (slice(g * quarter, (g + 1) * quarter), slice(h * LANES, (h + 1) * LANES))
                out[where] = jnp.where((column >> 2) == b, got, out[where])

    n_block = cols // BLOCK
    out[...] = jnp.zeros_like(out)

    @pl.when(left_second & jnp.logical_not(low_helper | high_helper))
    def _():
        pl.semaphore_wait(side_in.at[0], 1)

    @pl.loop(0, n_block)
    def _(b):
        for q, (start, width) in enumerate(CHUNKS):

            @pl.when(b * BLOCK == start)
            def _(q=q, start=start, width=width):
                landed = buf.at[:, pl.ds(start, width)]
                pltpu.make_async_copy(landed, landed, recv_sem.at[q]).wait()

        columns = [b * BLOCK + c for c in range(BLOCK)]
        data, signal = [], []
        for c in columns:
            block = buf[:, c].astype(jnp.float32)
            data.append(block.reshape(-1, rows).astype(jnp.bfloat16))
        summed = jnp.dot(
            trace_bf[...], jnp.concatenate(data, axis=1), preferred_element_type=jnp.float32
        )
        for i, c in enumerate(columns):
            _, _, inside = box_of(c)
            signal.append(
                jnp.where(inside, summed[:, i * rows : (i + 1) * rows] * inverse_at[...], -jnp.inf)
            )
        signal = jnp.concatenate(signal, axis=1)
        signal = [signal[g * slots : (g + 1) * slots] for g in range(GROUPS)]
        wide = lambda ref: jnp.concatenate([ref[c] for c in columns], axis=1)
        now = [None] * GROUPS
        parts = [None, (wide(later_high), wide(later_low))]
        mixed = wide(first_mixed)
        for step in range(SWEEPS * GROUPS):
            g = step % GROUPS
            if step > 0:
                mixed = older + multiply_part(g, 1 - g, parts[1 - g])
            if step + 1 < SWEEPS * GROUPS:
                older = multiply_part(1 - g, 1 - g, parts[1 - g])
            now[g] = jnp.maximum(signal[g] - mixed, 0.0)
            parts[g] = split(now[g])
        done = jnp.concatenate(now, axis=0)
        left_piece[b] = take_back(done, 0)

        @pl.when(has_left)
        def _():
            back(b).start()

        place_back(b, take_back(done, 1))

    @pl.when(has_right)
    def _():
        for copy in (side_fp, side_tr, side_meta):
            copy.wait_send()

    @pl.when(jnp.logical_not(has_right))
    def _():
        ret_piece[...] = jnp.zeros_like(ret_piece)

    @pl.loop(0, n_block)
    def _(b):
        @pl.when(has_right)
        def _():
            back(b).wait_recv()

        place_back(n_block + b, ret_piece[b])

    for q, (c0, n) in enumerate(CHUNKS):
        gone_out = buf.at[pl.ds(0, n_plane - 1), pl.ds(c0, n)]
        pltpu.make_async_copy(gone_out, gone_out, send_sem.at[q]).wait()

    @pl.when(has_left)
    def _():
        for b in range(n_block):
            back(b).wait_send()


def body(slab_data, footprints, traces, corners, counts):
    n_tile, n_plane = lax.axis_size("tile"), lax.axis_size("plane")
    cols, frames, rows = slab_data.shape
    rows = rows // n_plane
    slots, box = footprints.shape
    span = traces.shape[1]
    both = 2 * slots
    hbm = pl.BlockSpec(memory_space=pltpu.HBM)
    vmem = pl.BlockSpec(memory_space=pltpu.VMEM)
    f32, bf16, i32 = jnp.float32, jnp.bfloat16, jnp.int32
    dma = pltpu.SemaphoreType.DMA
    regular = pltpu.SemaphoreType.REGULAR
    return pl.pallas_call(
        functools.partial(kernel, n_tile, n_plane),
        out_shape=pltpu.VMEM((slots, box), f32),
        in_specs=[hbm] * 5,
        out_specs=vmem,
        scratch_shapes=[
            pltpu.VMEM((n_plane, cols, frames, rows), bf16),
            pltpu.VMEM((slots, box), f32),
            pltpu.VMEM((slots, box), f32),
            pltpu.VMEM((slots, span), f32),
            pltpu.VMEM((slots, span), f32),
            pltpu.VMEM((2, slots), i32),
            pltpu.VMEM((8, 128), i32),
            pltpu.VMEM((8, 128), i32),
            pltpu.SMEM((1, 1), i32),
            pltpu.VMEM((both, box), f32),
            pltpu.VMEM((cols, slots, rows), f32),
            pltpu.VMEM((cols, slots, rows), bf16),
            pltpu.VMEM((cols, slots, rows), bf16),
            pltpu.VMEM((both, rows), i32),
            pltpu.VMEM((both, rows), i32),
            pltpu.VMEM((both, LANES), i32),
            pltpu.VMEM((both, rows), f32),
            pltpu.VMEM((GROUPS, both, 2 * both), bf16),
            pltpu.VMEM((GROUPS, both, 2 * both), bf16),
            pltpu.VMEM((both, span), bf16),
            pltpu.VMEM((cols // BLOCK, slots // GROUPS, LANES), f32),
            pltpu.VMEM((cols // BLOCK, slots // GROUPS, LANES), f32),
            dma((4,)),
            dma((len(CHUNKS),)),
            dma((len(CHUNKS),)),
            dma((3,)),
            dma((3,)),
            dma((cols // BLOCK,)),
            dma((cols // BLOCK,)),
            regular((n_plane,)),
            regular((2,)),
            regular((n_plane // 8,)),
        ],
        compiler_params=pltpu.CompilerParams(
            collective_id=0, has_side_effects=True, vmem_limit_bytes=60 << 20
        ),
    )(slab_data, footprints, traces, corners.T, counts.reshape(1, 1))


def solution(mesh):
    in_specs = (
        P("tile", "plane", None),
        P(("tile", "plane"), None),
        P(("tile", "plane"), None),
        P(("tile", "plane"), None),
        P(("tile", "plane")),
    )
    out_specs = P(("tile", "plane"), None)
    return jax.shard_map(body, mesh=mesh, in_specs=in_specs, out_specs=out_specs, check_vma=False)
```

```python
import functools

import jax
import jax.numpy as jnp
from jax import lax
from jax.experimental import pallas as pl
from jax.experimental.pallas import tpu as pltpu
from jax.sharding import PartitionSpec as P

PR = 16
PC = 16
SWEEPS = 2
GROUPS = 2
CHUNKS = ((0, 8), (8, 4), (12, 4))
BLOCK = 4
X_SIZE = 4
LANES = 128
MESH = pl.DeviceIdType.MESH
GONE = 1 << 14


def mixed_order(left, own):
    half = own.shape[0] // GROUPS
    parts = []
    for g in range(GROUPS):
        parts += [left[g * half : (g + 1) * half], own[g * half : (g + 1) * half]]
    return jnp.concatenate(parts, axis=0)


def column_of(row):
    n = row.shape[1]
    eye = lax.broadcasted_iota(jnp.int32, (n, n), 0) == lax.broadcasted_iota(jnp.int32, (n, n), 1)
    spread = jnp.where(eye, jnp.broadcast_to(row.astype(jnp.float32), (n, n)), 0.0)
    return jnp.sum(spread, axis=1, keepdims=True).astype(jnp.int32)


def split(x):
    high = x.astype(jnp.bfloat16)
    return high, (x - high.astype(jnp.float32)).astype(jnp.bfloat16)


def kernel(
    n_tile, n_plane, slab, fp, tr, corners, counts, out,
    buf, own_fp, nb_fp, own_tr, nb_tr, own_corner, own_meta, nb_meta, own_count,
    patch, first_mixed, later_high, later_low, row_at, first_at, pick_at, inverse_at,
    weights, half_weights, trace_bf, own_piece, left_piece, ret_piece,
    load_sem, send_sem, recv_sem, side_send, side_recv, ret_send, ret_recv, plane_in, side_in, relay,
):
    cols, rows = buf.shape[1], buf.shape[3]
    slots = own_fp.shape[0]
    both = 2 * slots
    quarter = slots // GROUPS
    tile, me = lax.axis_index("tile"), lax.axis_index("plane")
    has_left, has_right = tile > 0, tile < n_tile - 1
    half = n_plane // 2
    place = jnp.where(me == 0, half - 1, jnp.where(me < half, me - 1, me))

    late = place >= half

    def plane_at(k):
        return jnp.where(k < half - 1, k + 1, jnp.where(k == half - 1, 0, k))

    left_first = has_left & (lax.rem(tile, X_SIZE) != 0)
    left_second = has_left & (lax.rem(tile, X_SIZE) == 0)
    right_second = has_right & (lax.rem(tile + 1, X_SIZE) != 0)
    right_first = has_right & (lax.rem(tile + 1, X_SIZE) == 0)

    barrier = pltpu.get_barrier_semaphore()

    @pl.loop(place + 1, n_plane)
    def _(k):
        pl.semaphore_signal(
            barrier, inc=1, device_id={"plane": plane_at(k)}, device_id_type=MESH
        )

    @pl.when(right_second)
    def _():
        pl.semaphore_signal(barrier, inc=1, device_id={"tile": tile + 1}, device_id_type=MESH)

    @pl.when(left_second & jnp.logical_not(late))
    def _():
        pl.semaphore_signal(barrier, inc=1, device_id={"tile": tile - 1}, device_id_type=MESH)

    loads = [
        pltpu.make_async_copy(src, dst, load_sem.at[i])
        for i, (src, dst) in enumerate(
            ((corners, own_corner), (counts, own_count), (tr, own_tr), (fp, own_fp))
        )
    ]
    for load in loads:
        load.start()
    right_told = right_first & jnp.logical_not(late)
    before = place + left_first.astype(jnp.int32) + right_told.astype(jnp.int32)

    @pl.when(before > 0)
    def _():
        pl.semaphore_wait(barrier, before)

    @pl.loop(0, place)
    def _(k):
        pl.semaphore_signal(
            plane_in.at[me], inc=1, device_id={"plane": plane_at(k)}, device_id_type=MESH
        )

    @pl.when(left_first)
    def _():
        pl.semaphore_signal(side_in.at[1], inc=1, device_id={"tile": tile - 1}, device_id_type=MESH)

    @pl.when(right_told)
    def _():
        pl.semaphore_signal(side_in.at[0], inc=1, device_id={"tile": tile + 1}, device_id_type=MESH)

    def send(q, peer):
        c0, n = CHUNKS[q]
        pltpu.make_async_remote_copy(
            slab.at[pl.ds(c0, n), :, pl.ds(pl.multiple_of(peer * rows, rows), rows)],
            buf.at[me, pl.ds(c0, n)],
            send_sem.at[q],
            recv_sem.at[q],
            device_id={"plane": peer},
            device_id_type=MESH,
        ).start()

    early = jnp.minimum(place, half)
    for a, b in ((0, 2), (2, half), (half, n_plane)):
        for q in range(len(CHUNKS)):

            @pl.loop(jnp.minimum(a, place), jnp.minimum(b, place))
            def _(k, q=q):
                send(q, jnp.where(late, k, plane_at(k)))

    for q, (c0, n) in enumerate(CHUNKS):
        pltpu.make_async_copy(
            slab.at[pl.ds(c0, n), :, pl.ds(pl.multiple_of(me * rows, rows), rows)],
            buf.at[me, pl.ds(c0, n)],
            recv_sem.at[q],
        ).start()

    def side(i, src, dst):
        return pltpu.make_async_remote_copy(
            src, dst, side_send.at[i], side_recv.at[i],
            device_id={"tile": tile + 1}, device_id_type=MESH,
        )

    side_fp, side_tr = side(0, fp, nb_fp), side(1, tr, nb_tr)
    side_meta = side(2, own_meta, nb_meta)
    loads[0].wait()
    loads[1].wait()
    lane = lax.broadcasted_iota(jnp.int32, (1, slots), 1)
    own_meta[...] = jnp.zeros_like(own_meta)
    own_meta[0:1, 0:slots] = own_corner[0:1, :]
    own_meta[1:2, 0:slots] = jnp.where(lane < own_count[0, 0], own_corner[1:2, :], GONE)

    @pl.when(right_second & jnp.logical_not(late))
    def _():
        pl.semaphore_wait(side_in.at[1], 1)

    @pl.when(has_right & jnp.logical_not(late))
    def _():
        side_meta.start()
        side_tr.start()
        side_fp.start()

    def send_to_later(low, high):
        @pl.loop(jnp.maximum(place + 1, low), jnp.maximum(place + 1, high))
        def _(k):
            peer = plane_at(k)
            pl.semaphore_wait(plane_in.at[peer], 1)
            for q in range(len(CHUNKS)):
                send(q, peer)

    quarter_planes = half // 2
    low_helper, high_helper = me < 2, (me >= half - 2) & (me < half)
    core = lax.rem(me, 2)

    def pass_on(helper):
        for i in range(quarter_planes // 2):

            @pl.when(helper & left_second)
            def _(i=i):
                if i == 0:
                    pl.semaphore_wait(side_in.at[0], 1)
                pl.semaphore_signal(
                    relay.at[i], inc=1, device_id={"tile": tile - 1}, device_id_type=MESH
                )

    def hand_on(helper, base):
        for i in range(quarter_planes // 2):

            @pl.when(helper & right_first)
            def _(i=i):
                pl.semaphore_wait(relay.at[i], 1)
                pl.semaphore_signal(
                    side_in.at[1], inc=1, device_id={"plane": base + 2 * i + core},
                    device_id_type=MESH,
                )

    send_to_later(0, half + quarter_planes)
    pass_on(high_helper)
    send_to_later(half + quarter_planes, n_plane)
    pass_on(low_helper)
    hand_on(high_helper, half)
    hand_on(low_helper, half + quarter_planes)

    @pl.when((right_second | right_first) & late)
    def _():
        pl.semaphore_wait(side_in.at[1], 1)

    @pl.when(right_first & late)
    def _():
        pl.semaphore_signal(side_in.at[0], inc=1, device_id={"tile": tile + 1}, device_id_type=MESH)

    @pl.when(has_right & late)
    def _():
        side_meta.start()
        side_tr.start()
        side_fp.start()

    loads[2].wait()
    loads[3].wait()

    @pl.when(has_left)
    def _():
        side_meta.wait_recv()
        side_tr.wait_recv()
        side_fp.wait_recv()

    @pl.when(jnp.logical_not(has_left))
    def _():
        nb_meta[...] = jnp.full(nb_meta.shape, GONE, jnp.int32)
        nb_tr[...] = jnp.zeros_like(nb_tr)
        nb_fp[...] = jnp.zeros_like(nb_fp)

    top = mixed_order(column_of(nb_meta[0:1, 0:slots]), column_of(own_meta[0:1, 0:slots]))
    first = mixed_order(
        column_of(nb_meta[1:2, 0:slots]) - cols, column_of(own_meta[1:2, 0:slots])
    )
    alive = first < cols
    patch[...] = mixed_order(nb_fp[...], own_fp[...])
    trace = mixed_order(nb_tr[...], own_tr[...])
    gram = lax.dot_general(
        trace, trace, (((1,), (1,)), ((), ())),
        precision=lax.Precision.HIGHEST, preferred_element_type=jnp.float32,
    )
    eye = lax.broadcasted_iota(jnp.int32, (both, both), 0) == lax.broadcasted_iota(
        jnp.int32, (both, both), 1
    )
    diagonal = jnp.sum(jnp.where(eye, gram, 0.0), axis=1, keepdims=True)
    scale = jnp.where(alive, diagonal, 1.0)
    high, low = split(jnp.where(eye, 0.0, gram) / scale)
    for g in range(GROUPS):
        at = slice(g * slots, (g + 1) * slots)
        weights[g, 0:slots, 0:both] = high[at]
        weights[g, 0:slots, both : 2 * both] = high[at]
        weights[g, slots:both, 0:both] = low[at]
        weights[g, slots:both, both : 2 * both] = jnp.zeros((slots, both), jnp.bfloat16)
        for of in range(GROUPS):
            src = slice(of * slots, (of + 1) * slots)
            a = of * both
            half_weights[g, 0:slots, a : a + slots] = high[at, src]
            half_weights[g, 0:slots, a + slots : a + both] = high[at, src]
            half_weights[g, slots:both, a : a + slots] = low[at, src]
            half_weights[g, slots:both, a + slots : a + both] = jnp.zeros(
                (slots, slots), jnp.bfloat16
            )
    trace_bf[...] = trace.astype(jnp.bfloat16)
    inverse_at[...] = jnp.broadcast_to(1.0 / scale, (both, rows))

    i_at = lax.broadcasted_iota(jnp.int32, (both, rows), 1) - top
    row_at[...] = jnp.where((i_at >= 0) & (i_at < PR), i_at, -1)
    first_at[...] = jnp.broadcast_to(first, (both, rows))
    lane_row = lax.broadcasted_iota(jnp.int32, (both, LANES), 1)
    pick_at[...] = jnp.broadcast_to(top, (both, LANES)) + (lane_row & (PR - 1))

    def box_of(c):
        i_of = row_at[...]
        j_of = c - first_at[...]
        return i_of, j_of, (i_of >= 0) & (j_of >= 0) & (j_of < PC)

    def multiply(g, parts):
        stacked = jnp.concatenate([p[0] for p in parts] + [p[1] for p in parts], axis=0)
        product = jnp.dot(weights[g], stacked, preferred_element_type=jnp.float32)
        return product[0:slots] + product[slots:both]

    def multiply_part(g, of, part):
        at = of * both
        stacked = jnp.concatenate(part, axis=0)
        product = jnp.dot(
            half_weights[g, :, at : at + both], stacked, preferred_element_type=jnp.float32
        )
        return product[0:slots] + product[slots:both]

    @pl.loop(0, cols // 2)
    def _(pair):
        highs, lows = [], []
        for c in (2 * pair, 2 * pair + 1):
            i_of, j_of, inside = box_of(c)
            at = (i_of & 7) * PC + (j_of & (PC - 1))
            lower = jnp.take_along_axis(patch[:, 0:LANES], at, axis=1)
            upper = jnp.take_along_axis(patch[:, LANES : 2 * LANES], at, axis=1)
            high, low = split(jnp.where(inside, jnp.where(i_of >= 8, upper, lower), 0.0))
            later_high[c] = high[slots:both]
            later_low[c] = low[slots:both]
            highs.append(high)
            lows.append(low)
        mixed = multiply(0, [(jnp.concatenate(highs, axis=1), jnp.concatenate(lows, axis=1))])
        first_mixed[2 * pair] = mixed[:, 0:rows]
        first_mixed[2 * pair + 1] = mixed[:, rows : 2 * rows]

    lane = lax.broadcasted_iota(jnp.int32, (quarter, LANES), 1)
    lane_spot = lane >> 4

    def take_back(c0, n, done, which, target):
        kept = target[c0 // BLOCK] if c0 % BLOCK else jnp.zeros((quarter, LANES), jnp.float32)
        for g in range(GROUPS):
            a = g * slots + which * quarter
            for c in range(n):
                got = jnp.take_along_axis(
                    done[a : a + quarter, c * rows : (c + 1) * rows],
                    pick_at[a : a + quarter, :],
                    axis=1,
                )
                kept = jnp.where(lane_spot == g * BLOCK + (c0 + c) % BLOCK, got, kept)
        target[c0 // BLOCK] = kept

    def back(b):
        return pltpu.make_async_remote_copy(
            left_piece.at[b], ret_piece.at[b], ret_send.at[b], ret_recv.at[b],
            device_id={"tile": tile - 1}, device_id_type=MESH,
        )

    def place_back(b, pieces, sofar):
        new = []
        for g in range(GROUPS):
            a = g * slots + quarter
            for h in range(2):
                column = first_at[a : a + quarter, :] + (lane & (PC - 1))
                at = g * (BLOCK * PR) + (column & (BLOCK - 1)) * PR + (lane >> 4) + 8 * h
                got = jnp.take_along_axis(pieces, at, axis=1)
                new.append(jnp.where((column >> 2) == b, got, sofar[g * 2 + h]))
        return new

    n_block = cols // BLOCK
    boxes = [jnp.zeros((quarter, LANES), jnp.float32)] * (2 * GROUPS)
    for c0 in range(0, cols, BLOCK):
        n = BLOCK
        for q, (start, width) in enumerate(CHUNKS):
            if start == c0:
                landed = buf.at[:, pl.ds(start, width)]
                pltpu.make_async_copy(landed, landed, recv_sem.at[q]).wait()
        data, signal = [], []
        for c in range(c0, c0 + n):
            block = buf[:, c].astype(jnp.float32)
            data.append(block.reshape(-1, rows).astype(jnp.bfloat16))
        summed = jnp.dot(
            trace_bf[...], jnp.concatenate(data, axis=1), preferred_element_type=jnp.float32
        )
        for c in range(n):
            _, _, inside = box_of(c0 + c)
            signal.append(
                jnp.where(inside, summed[:, c * rows : (c + 1) * rows] * inverse_at[...], -jnp.inf)
            )
        signal = jnp.concatenate(signal, axis=1)
        signal = [signal[g * slots : (g + 1) * slots] for g in range(GROUPS)]
        wide = lambda ref: jnp.concatenate([ref[c] for c in range(c0, c0 + n)], axis=1)
        now = [None] * GROUPS
        parts = [None] + [(wide(later_high), wide(later_low))]
        mixed = wide(first_mixed)
        for step in range(SWEEPS * GROUPS):
            g = step % GROUPS
            if step > 0:
                mixed = older + multiply_part(g, 1 - g, parts[1 - g])
            if step + 1 < SWEEPS * GROUPS:
                older = multiply_part(1 - g, 1 - g, parts[1 - g])
            now[g] = jnp.maximum(signal[g] - mixed, 0.0)
            parts[g] = split(now[g])
        done = jnp.concatenate(now, axis=0)
        if True:
            take_back(c0, n, done, 0, left_piece)
        if c0 == 0:

            @pl.when(left_second & jnp.logical_not(low_helper | high_helper))
            def _():
                pl.semaphore_wait(side_in.at[0], 1)

        if (c0 + n) % BLOCK == 0:

            @pl.when(has_left)
            def _(b=c0 // BLOCK):
                back(b).start()

        take_back(c0, n, done, 1, own_piece)
        if (c0 + n) % BLOCK == 0:
            boxes = place_back(c0 // BLOCK, own_piece[c0 // BLOCK], boxes)

    @pl.when(has_right)
    def _():
        for copy in (side_fp, side_tr, side_meta):
            copy.wait_send()

    @pl.when(jnp.logical_not(has_right))
    def _():
        ret_piece[...] = jnp.zeros_like(ret_piece)

    for b in range(n_block):

        @pl.when(has_right)
        def _(b=b):
            back(b).wait_recv()

        boxes = place_back(n_block + b, ret_piece[b], boxes)
    for g in range(GROUPS):
        for h in range(2):
            out[g * quarter : (g + 1) * quarter, h * LANES : (h + 1) * LANES] = boxes[g * 2 + h]

    for q, (c0, n) in enumerate(CHUNKS):
        gone_out = buf.at[pl.ds(0, n_plane - 1), pl.ds(c0, n)]
        pltpu.make_async_copy(gone_out, gone_out, send_sem.at[q]).wait()

    @pl.when(has_left)
    def _():
        for b in range(n_block):
            back(b).wait_send()


def body(slab_data, footprints, traces, corners, counts):
    n_tile, n_plane = lax.axis_size("tile"), lax.axis_size("plane")
    cols, frames, rows = slab_data.shape
    rows = rows // n_plane
    slots, box = footprints.shape
    span = traces.shape[1]
    both = 2 * slots
    hbm = pl.BlockSpec(memory_space=pltpu.HBM)
    vmem = pl.BlockSpec(memory_space=pltpu.VMEM)
    f32, bf16, i32 = jnp.float32, jnp.bfloat16, jnp.int32
    dma = pltpu.SemaphoreType.DMA
    regular = pltpu.SemaphoreType.REGULAR
    return pl.pallas_call(
        functools.partial(kernel, n_tile, n_plane),
        out_shape=pltpu.VMEM((slots, box), f32),
        in_specs=[hbm] * 5,
        out_specs=vmem,
        scratch_shapes=[
            pltpu.VMEM((n_plane, cols, frames, rows), bf16),
            pltpu.VMEM((slots, box), f32),
            pltpu.VMEM((slots, box), f32),
            pltpu.VMEM((slots, span), f32),
            pltpu.VMEM((slots, span), f32),
            pltpu.VMEM((2, slots), i32),
            pltpu.VMEM((8, 128), i32),
            pltpu.VMEM((8, 128), i32),
            pltpu.SMEM((1, 1), i32),
            pltpu.VMEM((both, box), f32),
            pltpu.VMEM((cols, slots, rows), f32),
            pltpu.VMEM((cols, slots, rows), bf16),
            pltpu.VMEM((cols, slots, rows), bf16),
            pltpu.VMEM((both, rows), i32),
            pltpu.VMEM((both, rows), i32),
            pltpu.VMEM((both, LANES), i32),
            pltpu.VMEM((both, rows), f32),
            pltpu.VMEM((GROUPS, both, 2 * both), bf16),
            pltpu.VMEM((GROUPS, both, 2 * both), bf16),
            pltpu.VMEM((both, span), bf16),
            pltpu.VMEM((cols // BLOCK, slots // GROUPS, LANES), f32),
            pltpu.VMEM((cols // BLOCK, slots // GROUPS, LANES), f32),
            pltpu.VMEM((cols // BLOCK, slots // GROUPS, LANES), f32),
            dma((4,)),
            dma((len(CHUNKS),)),
            dma((len(CHUNKS),)),
            dma((3,)),
            dma((3,)),
            dma((cols // BLOCK,)),
            dma((cols // BLOCK,)),
            regular((n_plane,)),
            regular((2,)),
            regular((n_plane // 8,)),
        ],
        compiler_params=pltpu.CompilerParams(
            collective_id=0, has_side_effects=True, vmem_limit_bytes=60 << 20
        ),
    )(slab_data, footprints, traces, corners.T, counts.reshape(1, 1))


def solution(mesh):
    in_specs = (
        P("tile", "plane", None),
        P(("tile", "plane"), None),
        P(("tile", "plane"), None),
        P(("tile", "plane"), None),
        P(("tile", "plane")),
    )
    out_specs = P(("tile", "plane"), None)
    return jax.shard_map(body, mesh=mesh, in_specs=in_specs, out_specs=out_specs, check_vma=False)
```
